32 devices in a mesh: seq: 8 (over z, x), head: 4 (over y, core).
Axes of the slice: x: 2, y: 2, z: 4, core: 2. Of those that a mesh axis runs over, the one named last changes fastest.
Arguments:
- queries: bfloat16 [8192, 2048], P('seq', 'head'), may hold values from -6 to 6
- key_rows: bfloat16 [8192, 2048], P('seq', 'head'), may hold values from -6 to 6
- value_rows: bfloat16 [8192, 4096], P('seq', 'head'), may hold values from -6 to 6
- out_gate: bfloat16 [8192, 4096], P('seq', 'head'), may hold values from -6 to 6
- write_rate: float32 [32, 8192], P('head', 'seq'), may hold values from 0.00390625 to 1
- log_gate: float32 [32, 8192], P('head', 'seq'), may hold values from -1 to 0, as said below
- doc_start: int32 [8192], P('seq'), may hold values 0 or 1
- norm_gain: float32 [128], replicated, may hold values from 0.1 to 1.9
- out_weight: bfloat16 [4096, 2048], P('head'), may hold values from -0.125 to 0.125
Outputs:
- mixed: bfloat16 [8192, 2048], P('seq', 'head')
The draws below stay inside these ranges and needn't reach their ends.
Inputs may be any that keep to these rules, and one draw needn't show every extreme that they name: `log_gate`: log of the per-token decay factor of each value head's state.
All inputs are finite; a program needn't handle non-finite values. No bound on the sum of `doc_start` on one device may be relied on, other than what follows from the above.
Results may differ from the reference program's by a relative error of at most 0.027.
Values may be sent and summed in bfloat16 or wider, within the bound.
No kernel may reach another device: no remote copies, remote signals or barrier semaphores. Data moves between devices by JAX's collectives and lax.ppermute only.
A program may use at most 128 MiB of HBM per device.

```python
import math
import jax
import jax.numpy as jnp
from jax import lax

D = 2048
VALUE_HEAD_COUNT = 32
HK = 16
DK = 128
DV = 128
SPAN = 64
TOK_DEV = 1024
SEQUENCE_TOKENS = 8192
N_HEAD = 4


def head_kinds(key):
    chooser = jax.random.uniform(jax.random.fold_in(key, 7), (VALUE_HEAD_COUNT, 1))
    fast_share = 0.35
    medium_share = 0.15
    fast_heads = chooser < fast_share
    medium_heads = (chooser >= fast_share) & (chooser < fast_share + medium_share)
    return (fast_heads, medium_heads)


def draw_write_rate(key, part):
    lanes = jax.random.split(jax.random.fold_in(key, 11), 2)
    fast_heads, medium_heads = head_kinds(key)
    strong_rates = jax.random.uniform(lanes[0], (VALUE_HEAD_COUNT, SEQUENCE_TOKENS), minval=0.05, maxval=1.0)
    lowest_rate = 0.25 * DK / SEQUENCE_TOKENS
    weak_rates = jnp.exp(jax.random.uniform(lanes[1], (VALUE_HEAD_COUNT, SEQUENCE_TOKENS), minval=math.log(lowest_rate), maxval=math.log(4.0 * lowest_rate)))
    chosen = jnp.where(fast_heads | medium_heads, strong_rates, weak_rates)
    return chosen.astype(jnp.float32)


def draw_log_gate(key, part):
    sequence_lanes = jax.random.split(jax.random.fold_in(key, 13), 7)
    fast_heads, medium_heads = head_kinds(key)
    fast_heads = fast_heads[:, :, None]
    slow_rate = jnp.exp(jax.random.uniform(sequence_lanes[1], (VALUE_HEAD_COUNT, 1, 1), minval=math.log(0.05 / SEQUENCE_TOKENS), maxval=math.log(1.0 / SEQUENCE_TOKENS)))
    fast_rate = jnp.exp(jax.random.uniform(sequence_lanes[2], (VALUE_HEAD_COUNT, 1, 1), minval=math.log(1.0 / 50.0), maxval=math.log(1.0 / 30.0)))
    base_rate = jnp.where(fast_heads, fast_rate, slow_rate)
    shard_factor = jnp.exp(jax.random.uniform(sequence_lanes[3], (VALUE_HEAD_COUNT, SEQUENCE_TOKENS // TOK_DEV, 1), minval=math.log(0.5), maxval=math.log(2.0)))
    token_factor = jnp.exp(jax.random.uniform(sequence_lanes[4], (VALUE_HEAD_COUNT, SEQUENCE_TOKENS // TOK_DEV, TOK_DEV), minval=math.log(0.5), maxval=math.log(2.0)))
    steady_decay_part = (base_rate * shard_factor * token_factor).reshape(VALUE_HEAD_COUNT, SEQUENCE_TOKENS)
    spike_token_index = jax.random.randint(sequence_lanes[5], (VALUE_HEAD_COUNT, 2, 1), 0, SEQUENCE_TOKENS)
    token_positions = jnp.arange(SEQUENCE_TOKENS, dtype=jnp.int32)
    spike_token_hits = jnp.any(token_positions[None, None, :] == spike_token_index, axis=1)
    spike_decay_keep = jax.random.uniform(sequence_lanes[6], (VALUE_HEAD_COUNT, SEQUENCE_TOKENS), minval=0.5, maxval=0.8)
    layer_output = -steady_decay_part + jnp.where(spike_token_hits, jnp.log(spike_decay_keep), 0.0)
    return layer_output.astype(jnp.float32)


def place_ends(values, key, low, top_value):
    longest = values.shape.index(max(values.shape))
    spots = []
    for shift in (0, 1):
        where = [jax.random.randint(jax.random.fold_in(key, axis), (), 0, length) for axis, length in enumerate(values.shape)]
        where[longest] = (where[longest] + shift) % values.shape[longest]
        spots.append(tuple(where))
    return values.at[spots[0]].set(low).at[spots[1]].set(top_value)


def raised(values, own_key, source, target, blocks, factor):
    def block_of(axis_at):
        return (jnp.arange(values.shape[axis_at]) // (values.shape[axis_at] // blocks)).reshape((-1,) + (1,) * (values.ndim - 1 - axis_at))

    near = jax.random.permutation(own_key, blocks)[block_of(target)]
    other_side = (block_of(target) + blocks // 2) % blocks
    return jnp.where((block_of(source) == near) | (block_of(source) == other_side), factor * values, values)


def levels(own_key, dims, cuts, smallest, high):
    loudness, own = 1.0, jax.random.fold_in(own_key, 6)
    for dim, blocks in cuts:
        draws = jnp.exp(jax.random.uniform(jax.random.fold_in(own, dim), (blocks,), jnp.float32, smallest / len(cuts), high / len(cuts)))
        loudness = loudness * jnp.repeat(draws, dims[dim] // blocks).reshape([-1 if axis == dim else 1 for axis in range(len(dims))])
    return loudness


def noise(own_key, shape, deviation, reach, cuts=(), kind=jnp.bfloat16):
    result = deviation * jax.random.normal(own_key, shape, jnp.float32)
    if cuts:
        result = result * levels(own_key, shape, cuts, -0.22, 0.18)
    return jnp.clip(result, -reach, reach).astype(kind)


def gaussian_with(key, shape, scale, bound, cuts, heavy, kind=jnp.bfloat16):
    drawn = scale * jax.random.normal(key, shape, jnp.float32)
    if cuts:
        drawn = drawn * levels(key, shape, cuts, -0.22, 0.18)
    return jnp.clip(raised(drawn, jax.random.fold_in(key, 3), *heavy), -bound, bound).astype(kind)


def setup_inputs(seed: int = 0) -> dict:
    seeds = jax.random.split(jax.random.key(seed), 10)
    return {
        "queries": noise(seeds[0], (SEQUENCE_TOKENS, HK * DK), 1.0, 6.0, ((0, 8), (1, 4))),
        "key_rows": noise(seeds[1], (SEQUENCE_TOKENS, HK * DK), 1.0, 6.0, ((0, 8), (1, 4))),
        "value_rows": noise(seeds[2], (SEQUENCE_TOKENS, VALUE_HEAD_COUNT * DV), 1.0, 6.0, ((0, 8), (1, 4))),
        "out_gate": noise(seeds[3], (SEQUENCE_TOKENS, VALUE_HEAD_COUNT * DV), 1.0, 6.0, ((0, 8), (1, 4))),
        "write_rate": draw_write_rate(jax.random.fold_in(seeds[9], 71), 0),
        "log_gate": draw_log_gate(jax.random.fold_in(seeds[9], 71), 0),
        "doc_start": place_ends((jax.random.randint(seeds[6], (SEQUENCE_TOKENS,), 0, 16 * TOK_DEV) < 1).astype(jnp.int32), jax.random.fold_in(seeds[6], 1), 0, 1),
        "norm_gain": jnp.clip(1.0 + 0.18 * jax.random.normal(seeds[7], (DV,), jnp.float32), 0.1, 1.9),
        "out_weight": gaussian_with(seeds[8], (VALUE_HEAD_COUNT * DV, D), (VALUE_HEAD_COUNT * DV) ** -0.5, 0.125, ((0, 4),), (0, 1, 4, 2.0)),
    }


highest = lax.Precision.HIGHEST

def unit_rows(values):
    return values * lax.rsqrt(lax.optimization_barrier(jnp.sum(values * values, axis=-1, keepdims=True)) + 1e-06)

def block_parts(queries, keys, values, rates, logs, starts):
    cumlog = jnp.cumsum(logs, axis=-1)
    resets = jnp.cumsum(starts, axis=-1)
    token_positions = jnp.arange(SPAN)
    lower_tri = token_positions[:, None] >= token_positions[None, :]
    same_doc = (resets[..., :, None] == resets[..., None, :]) & lower_tri
    log_gap = cumlog[..., :, None] - cumlog[..., None, :]
    decays = jnp.where(same_doc, jnp.exp(jnp.where(same_doc, log_gap, 0.0)), 0.0)
    last_log = cumlog[..., -1:]
    head_keep = jnp.exp(cumlog) * (resets == 0.0)
    tail_keep = jnp.exp(last_log - cumlog) * (resets == resets[..., -1:])
    whole_keep = jnp.exp(cumlog[..., -1]) * (resets[..., -1] == 0.0)
    identity = jnp.eye(SPAN, dtype=jnp.float32)
    key_inner = jnp.einsum('...ik,...jk->...ij', keys, keys, precision=highest)
    coupling = rates[..., :, None] * key_inner * decays * (1.0 - identity)
    inverse = identity - coupling
    powered = coupling
    extent = 1
    while 2 * extent < SPAN:
        powered = jnp.matmul(powered, powered, precision=highest)
        inverse = jnp.matmul(inverse, identity + powered, precision=highest)
        extent = extent * 2
    erase_keys = jnp.matmul(inverse, (rates * head_keep)[..., None] * keys, precision=highest)
    write_vals = jnp.matmul(inverse, rates[..., None] * values, precision=highest)
    scores = jnp.einsum('...ik,...jk->...ij', queries, keys, precision=highest) * decays
    return (queries, keys, erase_keys, write_vals, scores, head_keep, tail_keep, whole_keep)

def state_terms(parts, states):
    queries, keys, erase_keys, write_vals, scores, head_keep, tail_keep, whole_keep = parts
    seen = jnp.einsum('...ck,...vk->...cv', queries, states, precision=highest)
    erased = jnp.einsum('...ck,...vk->...cv', erase_keys, states, precision=highest)
    return (head_keep[..., None] * seen - jnp.matmul(scores, erased, precision=highest), erased)

def block_step(parts, state_now):
    queries, keys, erase_keys, write_vals, scores, head_keep, tail_keep, whole_keep = parts
    terms, erased = state_terms(parts, state_now)
    output = terms + jnp.matmul(scores, write_vals, precision=highest)
    fresh_vals = write_vals - erased
    state_next = whole_keep[..., None, None] * state_now + jnp.einsum('...cv,...ck->...vk', tail_keep[..., None] * fresh_vals, keys, precision=highest)
    return (output, state_next)

def reference(queries, key_rows, value_rows, out_gate, write_rate, log_gate, doc_start, norm_gain, out_weight):
    per_key = VALUE_HEAD_COUNT // HK
    blocks = SEQUENCE_TOKENS // SPAN
    query_unit = unit_rows(queries.astype(jnp.float32).reshape(SEQUENCE_TOKENS, HK, DK))
    key_unit = unit_rows(key_rows.astype(jnp.float32).reshape(SEQUENCE_TOKENS, HK, DK))
    value_all = value_rows.astype(jnp.float32).reshape(SEQUENCE_TOKENS, VALUE_HEAD_COUNT, DV)
    starts = doc_start.astype(jnp.float32).reshape(blocks, SPAN)

    def one_head(head_index):
        key_index = head_index // per_key
        query_head = jnp.take(query_unit, key_index, axis=1).reshape(blocks, SPAN, DK)
        key_head = jnp.take(key_unit, key_index, axis=1).reshape(blocks, SPAN, DK)
        value_head = jnp.take(value_all, head_index, axis=1).reshape(blocks, SPAN, DV)
        rates = jnp.take(write_rate, head_index, axis=0).reshape(blocks, SPAN)
        logs = jnp.take(log_gate, head_index, axis=0).reshape(blocks, SPAN)
        parts = block_parts(query_head, key_head, value_head, rates, logs, starts)

        def advance(state_now, inputs_now):
            output, state_next = block_step(inputs_now, state_now)
            return (state_next, output)
        final_state, outputs = lax.scan(advance, jnp.zeros((DV, DK), jnp.float32), parts)
        return outputs.reshape(SEQUENCE_TOKENS, DV)
    attended = jnp.transpose(lax.map(one_head, jnp.arange(VALUE_HEAD_COUNT, dtype=jnp.int32)), (1, 0, 2))
    gate_vals = out_gate.astype(jnp.float32).reshape(SEQUENCE_TOKENS, VALUE_HEAD_COUNT, DV)
    scale_rows = lax.rsqrt(lax.optimization_barrier(jnp.mean(attended * attended, axis=-1, keepdims=True)) + 1e-06)
    normed = (attended * scale_rows * norm_gain * jax.nn.silu(gate_vals)).astype(jnp.bfloat16)
    normed = normed.reshape(SEQUENCE_TOKENS, VALUE_HEAD_COUNT * DV)
    group_rows = VALUE_HEAD_COUNT * DV // N_HEAD

    def add_group(total, group_index):
        piece = lax.dynamic_slice_in_dim(normed, group_index * group_rows, group_rows, 1)
        weight_rows = lax.dynamic_slice_in_dim(out_weight, group_index * group_rows, group_rows, 0)
        partial_sum = jnp.dot(piece, weight_rows, preferred_element_type=jnp.float32).astype(jnp.bfloat16)
        partial_sum = lax.optimization_barrier(partial_sum)
        return (total + partial_sum.astype(jnp.float32), None)
    mixed, unused = lax.scan(add_group, jnp.zeros((SEQUENCE_TOKENS, D), jnp.float32), jnp.arange(N_HEAD, dtype=jnp.int32))
    return mixed.astype(jnp.bfloat16)
```

```python
import functools

import jax
import jax.numpy as jnp
from jax import lax
from jax.experimental import pallas as pl
from jax.experimental.pallas import tpu as pltpu
from jax.sharding import PartitionSpec as P

DK = 128
DV = 128
BLK = 128
EPS = 1e-06
FAR = -1e30
F32 = jnp.float32
BF16 = jnp.bfloat16
MIB = 1024 * 1024


def dot(a, b):
    return jnp.dot(a, b, preferred_element_type=F32)


def dot_t(a, b):
    return lax.dot_general(a, b, (((1,), (1,)), ((), ())), preferred_element_type=F32)


def running_sum(values):
    lane = lax.broadcasted_iota(jnp.int32, values.shape, 1)
    step = 1
    while step < BLK:
        values = values + jnp.where(lane >= step, pltpu.roll(values, step, 1), 0.0)
        step *= 2
    return values


def columns_of(rows):
    pad = BLK - rows.shape[0]
    return jnp.transpose(jnp.concatenate([rows, jnp.zeros((pad, BLK), F32)], axis=0))


def doc_mask(reset_col, reset_row, strict):
    i = lax.broadcasted_iota(jnp.int32, (BLK, BLK), 0)
    j = lax.broadcasted_iota(jnp.int32, (BLK, BLK), 1)
    below = (i > j) if strict else (i >= j)
    return jnp.where(below & (reset_col == reset_row), 0.0, FAR)


def merge_masks():
    i = lax.broadcasted_iota(jnp.int32, (BLK, BLK), 0)
    j = lax.broadcasted_iota(jnp.int32, (BLK, BLK), 1)
    masks = []
    size = 1
    while size < BLK:
        same_pair = (i // (2 * size)) == (j // (2 * size))
        masks.append(same_pair & ((i // size) % 2 == 1) & ((j // size) % 2 == 0))
        size *= 2
    return masks, i == j


def shard_kernel(
    per_key, blocks, keys_here,
    log_ref, rate_ref, start_ref, k_ref, v_ref,
    wu_ref, zc_ref, rows_ref, end_ref,
    logs, rates, norms, kt, mask, db, keep, state,
):
    key = pl.program_id(0)
    count = per_key * blocks
    for k in range(keys_here):

        @pl.when(key == k)
        def _():
            for h in range(per_key):
                head = k * per_key + h
                for c in range(blocks):
                    at = h * blocks + c
                    span = slice(c * BLK, (c + 1) * BLK)
                    logs[at : at + 1, :] = log_ref[head : head + 1, span]
                    rates[at : at + 1, :] = rate_ref[head : head + 1, span]

    starts = start_ref[...].astype(F32)
    sums = running_sum(jnp.concatenate([logs[...], starts], axis=0))
    cum, reset = sums[:count], sums[count:]

    for c in range(blocks):
        flipped = jnp.transpose(k_ref[c * BLK : (c + 1) * BLK, :].astype(F32))
        kt[c] = flipped.astype(BF16)
        norms[c : c + 1, :] = jnp.sum(flipped * flipped, axis=0, keepdims=True)

    @pl.when(key == 0)
    def _():
        reset_cols = columns_of(reset)
        for c in range(blocks):
            mask[c] = doc_mask(reset_cols[:, c : c + 1], reset[c : c + 1, :], True)

    scale = lax.rsqrt(norms[...] + EPS)
    log_scale = jnp.concatenate([-0.5 * jnp.log(norms[...] + EPS)] * per_key, axis=0)
    scale = jnp.concatenate([scale] * per_key, axis=0)
    resets = jnp.concatenate([reset] * per_key, axis=0)
    rate = rates[...]
    last = cum[:, BLK - 1 :]
    last_reset = resets[:, BLK - 1 :]
    left_cols = columns_of(cum + jnp.log(rate) + log_scale)
    right = cum - log_scale
    head_keep = jnp.where(resets == 0.0, jnp.exp(cum), 0.0)
    tail = jnp.where(resets == last_reset, jnp.exp(last - cum), 0.0) * scale
    erase_row = rate * head_keep * scale
    whole = jnp.where(last_reset == 0.0, jnp.exp(last), 0.0)
    whole = jnp.broadcast_to(whole, (count, BLK))
    for at in range(count):
        keep[key * count + at] = whole[at : at + 1, :]
    rows_ref[0, 0:count, :] = cum
    rows_ref[0, count : 2 * count, :] = right
    rows_ref[0, 2 * count :, :] = reset

    masks, diag = merge_masks()
    inner = [dot(k_ref[c * BLK : (c + 1) * BLK, :], kt[c]) for c in range(blocks)]
    lower = []
    for at in range(count):
        c = at % blocks
        gap = left_cols[:, at : at + 1] - right[at : at + 1, :] + mask[c]
        lower.append(inner[c] * jnp.exp(gap))
    inverse = [jnp.where(diag, 1.0, 0.0) - jnp.where(masks[0], m, 0.0) for m in lower]
    lower = [m.astype(BF16) for m in lower]
    for level in masks[1:]:
        edge = [jnp.where(level, m, jnp.zeros_like(m)) for m in lower]
        now = [t.astype(BF16) for t in inverse]
        half = [dot(t, e).astype(BF16) for t, e in zip(now, edge)]
        inverse = [t - dot(f, b) for t, f, b in zip(inverse, half, now)]
    for at in range(count):
        c, h = at % blocks, at // blocks
        span = slice(c * BLK, (c + 1) * BLK)
        t = inverse[at]
        erase = dot((t * erase_row[at : at + 1, :]).astype(BF16), k_ref[span, :])
        write = dot((t * rate[at : at + 1, :]).astype(BF16), v_ref[span, h * DV : (h + 1) * DV])
        wu_ref[at, :, :DK] = erase.astype(BF16)
        wu_ref[at, :, DK:] = write.astype(BF16)
    for at in range(count):
        c = at % blocks
        tailed = (kt[c].astype(F32) * tail[at : at + 1, :]).astype(BF16)
        db[key * count + at] = dot(tailed, wu_ref[at]).astype(BF16)

    @pl.when(key == keys_here - 1)
    def _():
        heads_here = per_key * keys_here
        i = lax.broadcasted_iota(jnp.int32, (DK, DK), 0)
        j = lax.broadcasted_iota(jnp.int32, (DK, DK), 1)
        for h in range(heads_here):
            state[h, :, :DV] = jnp.zeros((DK, DV), F32)
            state[h, :, DV:] = jnp.where(i == j, 1.0, 0.0)

        def advance(c, carry):
            for h in range(heads_here):
                now = state[h]
                low = now.astype(BF16)
                zc_ref[h, c] = low
                at = h * blocks + c
                moved = dot(db[at, :, :DK], low)
                g = keep[at]
                state[h, :, :DV] = g * now[:, :DV] - moved[:, :DV] + db[at, :, DK:].astype(F32)
                state[h, :, DV:] = g * now[:, DV:] - moved[:, DV:]
            return carry

        lax.fori_loop(0, blocks, advance, 0)
        for h in range(heads_here):
            end_ref[h] = state[h].astype(BF16)


def shard_pass(log_gate, write_rate, starts, key_rows, value_rows, per_key):
    tokens_here = key_rows.shape[0]
    keys_here = key_rows.shape[1] // DK
    heads_here = keys_here * per_key
    blocks = tokens_here // BLK
    count = per_key * blocks
    wide = DK + DV
    whole = lambda *shape: pl.BlockSpec(shape, lambda key: (0,) * len(shape))
    return pl.pallas_call(
        functools.partial(shard_kernel, per_key, blocks, keys_here),
        grid=(keys_here,),
        in_specs=[
            whole(heads_here, tokens_here),
            whole(heads_here, tokens_here),
            whole(blocks, BLK),
            pl.BlockSpec((tokens_here, DK), lambda key: (0, key)),
            pl.BlockSpec((tokens_here, per_key * DV), lambda key: (0, key)),
        ],
        out_specs=[
            pl.BlockSpec((count, BLK, wide), lambda key: (key, 0, 0)),
            whole(heads_here, blocks, DK, wide),
            pl.BlockSpec((1, 2 * count + blocks, BLK), lambda key: (key, 0, 0)),
            whole(heads_here, DK, wide),
        ],
        out_shape=[
            jax.ShapeDtypeStruct((keys_here * count, BLK, wide), BF16),
            jax.ShapeDtypeStruct((heads_here, blocks, DK, wide), BF16),
            jax.ShapeDtypeStruct((keys_here, 2 * count + blocks, BLK), F32),
            jax.ShapeDtypeStruct((heads_here, DK, wide), BF16),
        ],
        scratch_shapes=[
            pltpu.VMEM((count, BLK), F32),
            pltpu.VMEM((count, BLK), F32),
            pltpu.VMEM((blocks, BLK), F32),
            pltpu.VMEM((blocks, DK, BLK), BF16),
            pltpu.VMEM((blocks, BLK, BLK), F32),
            pltpu.VMEM((keys_here * count, DK, wide), BF16),
            pltpu.VMEM((keys_here * count, 1, BLK), F32),
            pltpu.VMEM((heads_here, DK, wide), F32),
        ],
        compiler_params=pltpu.CompilerParams(vmem_limit_bytes=48 * MIB),
        cost_estimate=pl.CostEstimate(
            flops=keys_here * count * 18 * 2 * BLK**3, bytes_accessed=12 * MIB, transcendentals=0
        ),
        name="shard_pass",
    )(log_gate, write_rate, starts, key_rows, value_rows)


def local_kernel(per_key, blocks, rows_ref, q_ref, k_ref, wu_ref, zc_ref, out_ref, carry_ref):
    count = per_key * blocks
    cum = rows_ref[0, 0:count, :]
    right = rows_ref[0, count : 2 * count, :]
    reset = rows_ref[0, 2 * count :, :]
    cols = columns_of(jnp.concatenate([cum, reset], axis=0))
    units, inner, masks = [], [], []
    for c in range(blocks):
        span = slice(c * BLK, (c + 1) * BLK)
        query = q_ref[span, :].astype(F32)
        units.append(jnp.sum(query * query, axis=1, keepdims=True) + EPS)
        inner.append(dot_t(q_ref[span, :], k_ref[span, :]))
        masks.append(doc_mask(cols[:, count + c : count + c + 1], reset[c : c + 1, :], False))
    scores = []
    for at in range(count):
        c = at % blocks
        left = cols[:, at : at + 1] - 0.5 * jnp.log(units[c])
        gap = left - right[at : at + 1, :] + masks[c]
        scores.append((inner[c] * jnp.exp(gap)).astype(BF16))
    seen = [dot(scores[at], wu_ref[at]) for at in range(count)]
    for at in range(count):
        c, h = at % blocks, at // blocks
        span = slice(c * BLK, (c + 1) * BLK)
        reset_col = cols[:, count + c : count + c + 1]
        keep = jnp.where(reset_col == 0.0, jnp.exp(cols[:, at : at + 1]), 0.0) * lax.rsqrt(units[c])
        g = (keep * q_ref[span, :].astype(F32) - seen[at][:, :DK]).astype(BF16)
        both = dot(g, zc_ref[h, c])
        out_ref[span, h * DV : (h + 1) * DV] = both[:, :DV] + seen[at][:, DK:]
        carry_ref[span, h * DK : (h + 1) * DK] = both[:, DV:].astype(BF16)


def local_pass(key, rows, queries, key_rows, wu, zc, per_key):
    tokens_here = queries.shape[0]
    blocks = tokens_here // BLK
    count = per_key * blocks
    wide = DK + DV
    return pl.pallas_call(
        functools.partial(local_kernel, per_key, blocks),
        grid=(1,),
        in_specs=[
            pl.BlockSpec((1, 2 * count + blocks, BLK), lambda i: (key, 0, 0)),
            pl.BlockSpec((tokens_here, DK), lambda i: (0, key)),
            pl.BlockSpec((tokens_here, DK), lambda i: (0, key)),
            pl.BlockSpec((count, BLK, wide), lambda i: (key, 0, 0)),
            pl.BlockSpec((per_key, blocks, DK, wide), lambda i: (key, 0, 0, 0)),
        ],
        out_specs=[
            pl.BlockSpec((tokens_here, per_key * DV), lambda i: (0, 0)),
            pl.BlockSpec((tokens_here, per_key * DK), lambda i: (0, 0)),
        ],
        out_shape=[
            jax.ShapeDtypeStruct((tokens_here, per_key * DV), F32),
            jax.ShapeDtypeStruct((tokens_here, per_key * DK), BF16),
        ],
        compiler_params=pltpu.CompilerParams(vmem_limit_bytes=32 * MIB),
        cost_estimate=pl.CostEstimate(
            flops=count * 8 * 2 * BLK**3, bytes_accessed=4 * MIB, transcendentals=0
        ),
        name="local_pass",
    )(rows, queries, key_rows, wu, zc)


def finish_kernel(
    per_key, keys_here, sends, order,
    me_ref, *refs,
):
    outs = refs[:keys_here]
    carries = refs[keys_here : 2 * keys_here]
    start_ref, gate_ref, gain_ref, weight_ref, send_ref, keep_ref, normed = refs[2 * keys_here :]
    step = pl.program_id(0)

    @pl.when(step == 0)
    def _():
        for key in range(keys_here):
            for h in range(per_key):
                head = key * per_key + h
                span = slice(h * DV, (h + 1) * DV)
                wide = slice(head * DV, (head + 1) * DV)
                seen = outs[key][:, span] + dot(carries[key][:, span], start_ref[head])
                spread = jnp.mean(seen * seen, axis=1, keepdims=True)
                gate = gate_ref[:, wide].astype(F32)
                gated = gain_ref[...] * (gate / (1.0 + jnp.exp(-gate)))
                normed[:, wide] = (seen * lax.rsqrt(spread + EPS) * gated).astype(BF16)

    part = dot(normed[...], weight_ref[...]).astype(BF16)

    @pl.when(step < sends)
    def _():
        send_ref[...] = part

    @pl.when(step >= sends)
    def _():
        keep_ref[...] = part


def bit_reversed(size):
    order = [0]
    bit = 1
    while bit < size:
        order = [p for p in order] + [p | bit for p in order]
        bit *= 2
    half = size // 2
    reach = []

    def split(group, bit):
        if len(group) == 1:
            return group
        return split([p for p in group if not p & bit], 2 * bit) + split(
            [p for p in group if p & bit], 2 * bit
        )

    return split(list(range(size)), 1)


def finish_pass(index, rows, me, outs, carries, start, out_gate, gain, weight, per_key, groups):
    heads_here = out_gate.shape[1] // DV
    keys_here = len(outs)
    columns = weight.shape[1] // groups
    order = bit_reversed(groups)
    half = groups // 2
    order = order[half:] + order[:half]

    def column_of(step, me_ref):
        place = order[0]
        for at in range(1, groups):
            place = jnp.where(step == at, order[at], place)
        return (0, me_ref[0] ^ place)

    per_head = pl.BlockSpec((rows, per_key * DV), lambda step, me_ref: (index, 0))
    grid_spec = pltpu.PrefetchScalarGridSpec(
        num_scalar_prefetch=1,
        grid=(groups,),
        in_specs=[per_head] * (2 * keys_here)
        + [
            pl.BlockSpec((heads_here, DK, DV), lambda step, me_ref: (0, 0, 0)),
            pl.BlockSpec((rows, heads_here * DV), lambda step, me_ref: (index, 0)),
            pl.BlockSpec((1, DV), lambda step, me_ref: (0, 0)),
            pl.BlockSpec((weight.shape[0], columns), column_of),
        ],
        out_specs=[
            pl.BlockSpec((rows, columns), lambda step, me_ref: (0, jnp.minimum(step, half - 1))),
            pl.BlockSpec((rows, columns), lambda step, me_ref: (0, jnp.maximum(step - half, 0))),
        ],
        scratch_shapes=[pltpu.VMEM((rows, heads_here * DV), BF16)],
    )
    return pl.pallas_call(
        functools.partial(finish_kernel, per_key, keys_here, half, order),
        grid_spec=grid_spec,
        out_shape=[jax.ShapeDtypeStruct((rows, half * columns), BF16)] * 2,
        compiler_params=pltpu.CompilerParams(vmem_limit_bytes=32 * MIB),
        cost_estimate=pl.CostEstimate(
            flops=2 * rows * weight.shape[0] * weight.shape[1],
            bytes_accessed=8 * MIB,
            transcendentals=0,
        ),
        name="finish_pass",
    )(me, *outs, *carries, start, out_gate, gain, weight)


def compose_kernel(wide, later_ref, earlier_ref, out_ref):
    for h in range(later_ref.shape[0]):
        later = later_ref[h]
        moved = dot(later[:, DV:], earlier_ref[h])
        out_ref[h, :, :DV] = (moved[:, :DV] + later[:, :DV].astype(F32)).astype(BF16)
        if wide:
            out_ref[h, :, DV:] = moved[:, DV:].astype(BF16)


def compose(later, earlier):
    return pl.pallas_call(
        functools.partial(compose_kernel, earlier.shape[2] > DV),
        out_shape=jax.ShapeDtypeStruct(earlier.shape, BF16),
        cost_estimate=pl.CostEstimate(
            flops=2 * earlier.size * DK, bytes_accessed=4 * earlier.size, transcendentals=0
        ),
        name="compose",
    )(later, earlier)


def route(axis, target):
    size = lax.axis_size(axis)
    return [(i, target(i)) for i in range(size) if target(i) is not None]


def start_states(end, work):
    size = lax.axis_size("seq")
    heads = end.shape[0]
    me = lax.axis_index("seq")
    if size == 8 and heads % 2 == 0:
        half = heads // 2
        odd = me % 2 == 1
        pair = me // 2
        mine = jnp.where(odd, end[half:], end[:half])
        theirs = jnp.where(odd, end[:half], end[half:])
        got = lax.ppermute(theirs, "seq", route("seq", lambda i: i ^ 1))
        mine, got = work(mine, got)
        first = jnp.where(odd, got, mine)
        second = jnp.where(odd, mine, got)
        both = compose(second, first)
        before = lax.ppermute(both, "seq", route("seq", lambda i: i + 2 if i < 6 else None))
        both, before = work(both, before)
        third = compose(both, before[:, :, :DV])
        near = lax.ppermute(third, "seq", [(2, 4), (3, 5)])
        far = lax.ppermute(third, "seq", [(2, 6), (3, 7)])
        before, (near, far) = work(before, (near, far))
        here = jnp.where(pair == 2, near, compose(before, far))
        then = compose(first, here)
        own = jnp.where(odd, then, here)
        other = jnp.where(odd, here, then)
        back = lax.ppermute(other, "seq", route("seq", lambda i: i ^ 1))
        own, back = work(own, back)
        return jnp.concatenate(
            [jnp.where(odd, back, own), jnp.where(odd, own, back)], axis=0
        )

    def hop(step, state):
        return lax.ppermute(
            compose(end, state), "seq", route("seq", lambda i: i + 1 if i + 1 < size else None)
        )

    return lax.fori_loop(0, size - 1, hop, jnp.zeros((heads, DK, DV), BF16))


def local(
    queries, key_rows, value_rows, out_gate, write_rate, log_gate, doc_start, norm_gain, out_weight
):
    tokens_here = queries.shape[0]
    heads_here = value_rows.shape[1] // DV
    keys_here = key_rows.shape[1] // DK
    per_key = heads_here // keys_here
    groups = lax.axis_size("head")
    starts = doc_start.reshape(tokens_here // BLK, BLK)
    wu, zc, rows, end = shard_pass(
        log_gate, write_rate, starts, key_rows, value_rows, per_key
    )
    outs, carries = [], []

    def work(ready, coming):
        key = len(outs)
        if key < keys_here:
            held, ready = lax.optimization_barrier((rows, ready))
            out, carry = local_pass(key, held, queries, key_rows, wu, zc, per_key)
            outs.append(out)
            carries.append(carry)
        return ready, coming

    start = start_states(end, work)
    while len(outs) < keys_here:
        work(start, start)

    me = lax.axis_index("head").reshape(1).astype(jnp.int32)
    chunks = 4
    rows_each = tokens_here // chunks
    pieces = []
    for index in range(chunks):
        send, keep = finish_pass(
            index, rows_each, me, outs, carries, start, out_gate,
            norm_gain.reshape(1, DV), out_weight, per_key, groups,
        )
        bit = 1
        while bit < groups:
            got = lax.ppermute(send, "head", route("head", lambda i: i ^ bit))
            total = keep.astype(F32) + got.astype(F32)
            bit *= 2
            if bit < groups:
                width = total.shape[1] // 2
                keep = total[:, :width]
                send = total[:, width:].astype(BF16)
            else:
                keep = total
        pieces.append(keep.astype(BF16))
    return jnp.concatenate(pieces, axis=0)


def solution(mesh):
    placed = (
        P("seq", "head"),
        P("seq", "head"),
        P("seq", "head"),
        P("seq", "head"),
        P("head", "seq"),
        P("head", "seq"),
        P("seq"),
        P(),
        P("head", None),
    )
    return jax.shard_map(
        local, mesh=mesh, in_specs=placed, out_specs=P("seq", "head"), check_vma=False
    )
```

```python
import functools

import jax
import jax.numpy as jnp
from jax import lax
from jax.experimental import pallas as pl
from jax.experimental.pallas import tpu as pltpu
from jax.sharding import PartitionSpec as P

DK = 128
DV = 128
BLK = 128
EPS = 1e-06
FAR = -1e30
F32 = jnp.float32
BF16 = jnp.bfloat16
MIB = 1024 * 1024


def dot(a, b):
    return jnp.dot(a, b, preferred_element_type=F32)


def dot_t(a, b):
    return lax.dot_general(a, b, (((1,), (1,)), ((), ())), preferred_element_type=F32)


def running_sum(values):
    lane = lax.broadcasted_iota(jnp.int32, values.shape, 1)
    step = 1
    while step < BLK:
        values = values + jnp.where(lane >= step, pltpu.roll(values, step, 1), 0.0)
        step *= 2
    return values


def columns_of(rows):
    pad = BLK - rows.shape[0]
    return jnp.transpose(jnp.concatenate([rows, jnp.zeros((pad, BLK), F32)], axis=0))


def doc_mask(reset_col, reset_row, strict):
    i = lax.broadcasted_iota(jnp.int32, (BLK, BLK), 0)
    j = lax.broadcasted_iota(jnp.int32, (BLK, BLK), 1)
    below = (i > j) if strict else (i >= j)
    return jnp.where(below & (reset_col == reset_row), 0.0, FAR)


def merge_masks():
    i = lax.broadcasted_iota(jnp.int32, (BLK, BLK), 0)
    j = lax.broadcasted_iota(jnp.int32, (BLK, BLK), 1)
    masks = []
    size = 1
    while size < BLK:
        same_pair = (i // (2 * size)) == (j // (2 * size))
        masks.append(same_pair & ((i // size) % 2 == 1) & ((j // size) % 2 == 0))
        size *= 2
    return masks, i == j


def shard_kernel(
    per_key, blocks, keys_here,
    me_ref, log_ref, rate_ref, start_ref, k_ref, v_ref,
    wu_ref, zc_ref, rows_ref, mine_ref, theirs_ref,
    logs, rates, norms, kt, mask, db, keep, state,
):
    key = pl.program_id(0)
    count = per_key * blocks
    for k in range(keys_here):

        @pl.when(key == k)
        def _():
            for h in range(per_key):
                head = k * per_key + h
                for c in range(blocks):
                    at = h * blocks + c
                    span = slice(c * BLK, (c + 1) * BLK)
                    logs[at : at + 1, :] = log_ref[head : head + 1, span]
                    rates[at : at + 1, :] = rate_ref[head : head + 1, span]

    starts = start_ref[...].astype(F32)
    sums = running_sum(jnp.concatenate([logs[...], starts], axis=0))
    cum, reset = sums[:count], sums[count:]

    for c in range(blocks):
        flipped = jnp.transpose(k_ref[c * BLK : (c + 1) * BLK, :].astype(F32))
        kt[c] = flipped.astype(BF16)
        norms[c : c + 1, :] = jnp.sum(flipped * flipped, axis=0, keepdims=True)

    @pl.when(key == 0)
    def _():
        reset_cols = columns_of(reset)
        for c in range(blocks):
            mask[c] = doc_mask(reset_cols[:, c : c + 1], reset[c : c + 1, :], True)

    scale = lax.rsqrt(norms[...] + EPS)
    log_scale = jnp.concatenate([-0.5 * jnp.log(norms[...] + EPS)] * per_key, axis=0)
    scale = jnp.concatenate([scale] * per_key, axis=0)
    resets = jnp.concatenate([reset] * per_key, axis=0)
    rate = rates[...]
    last = cum[:, BLK - 1 :]
    last_reset = resets[:, BLK - 1 :]
    left_cols = columns_of(cum + jnp.log(rate) + log_scale)
    right = cum - log_scale
    head_keep = jnp.where(resets == 0.0, jnp.exp(cum), 0.0)
    tail = jnp.where(resets == last_reset, jnp.exp(last - cum), 0.0) * scale
    erase_row = rate * head_keep * scale
    whole = jnp.where(last_reset == 0.0, jnp.exp(last), 0.0)
    whole = jnp.broadcast_to(whole, (count, BLK))
    for at in range(count):
        keep[key * count + at] = whole[at : at + 1, :]
    rows_ref[0, 0:count, :] = cum
    rows_ref[0, count : 2 * count, :] = right
    rows_ref[0, 2 * count :, :] = reset

    masks, diag = merge_masks()
    inner = [dot(k_ref[c * BLK : (c + 1) * BLK, :], kt[c]) for c in range(blocks)]
    lower = []
    for at in range(count):
        c = at % blocks
        gap = left_cols[:, at : at + 1] - right[at : at + 1, :] + mask[c]
        lower.append(inner[c] * jnp.exp(gap))
    inverse = [jnp.where(diag, 1.0, 0.0) - jnp.where(masks[0], m, 0.0) for m in lower]
    lower = [m.astype(BF16) for m in lower]
    for level in masks[1:]:
        edge = [jnp.where(level, m, jnp.zeros_like(m)) for m in lower]
        now = [t.astype(BF16) for t in inverse]
        half = [dot(t, e).astype(BF16) for t, e in zip(now, edge)]
        inverse = [t - dot(f, b) for t, f, b in zip(inverse, half, now)]
    for at in range(count):
        c, h = at % blocks, at // blocks
        span = slice(c * BLK, (c + 1) * BLK)
        t = inverse[at]
        erase = dot((t * erase_row[at : at + 1, :]).astype(BF16), k_ref[span, :])
        write = dot((t * rate[at : at + 1, :]).astype(BF16), v_ref[span, h * DV : (h + 1) * DV])
        wu_ref[at, :, :DK] = erase.astype(BF16)
        wu_ref[at, :, DK:] = write.astype(BF16)
    for at in range(count):
        c = at % blocks
        tailed = (kt[c].astype(F32) * tail[at : at + 1, :]).astype(BF16)
        db[key * count + at] = dot(tailed, wu_ref[at]).astype(BF16)

    @pl.when(key == keys_here - 1)
    def _():
        heads_here = per_key * keys_here
        i = lax.broadcasted_iota(jnp.int32, (DK, DK), 0)
        j = lax.broadcasted_iota(jnp.int32, (DK, DK), 1)
        for h in range(heads_here):
            state[h, :, :DV] = jnp.zeros((DK, DV), F32)
            state[h, :, DV:] = jnp.where(i == j, 1.0, 0.0)

        def advance(c, carry):
            for h in range(heads_here):
                now = state[h]
                low = now.astype(BF16)
                zc_ref[h, c] = low
                at = h * blocks + c
                moved = dot(db[at, :, :DK], low)
                g = keep[at]
                state[h, :, :DV] = g * now[:, :DV] - moved[:, :DV] + db[at, :, DK:].astype(F32)
                state[h, :, DV:] = g * now[:, DV:] - moved[:, DV:]
            return carry

        lax.fori_loop(0, blocks, advance, 0)
        half = mine_ref.shape[0]
        odd = lax.rem(me_ref[0], 2) == 1
        for h in range(heads_here):
            ends = state[h].astype(BF16)
            ours = odd if h >= half else jnp.logical_not(odd)

            @pl.when(ours)
            def _():
                mine_ref[h % half] = ends

            @pl.when(jnp.logical_not(ours))
            def _():
                theirs_ref[h % half] = ends


def shard_pass(me, log_gate, write_rate, starts, key_rows, value_rows, per_key):
    tokens_here = key_rows.shape[0]
    keys_here = key_rows.shape[1] // DK
    heads_here = keys_here * per_key
    blocks = tokens_here // BLK
    count = per_key * blocks
    wide = DK + DV
    whole = lambda *shape: pl.BlockSpec(shape, lambda key: (0,) * len(shape))
    return pl.pallas_call(
        functools.partial(shard_kernel, per_key, blocks, keys_here),
        grid=(keys_here,),
        in_specs=[
            pl.BlockSpec(memory_space=pltpu.SMEM),
            whole(heads_here, tokens_here),
            whole(heads_here, tokens_here),
            whole(blocks, BLK),
            pl.BlockSpec((tokens_here, DK), lambda key: (0, key)),
            pl.BlockSpec((tokens_here, per_key * DV), lambda key: (0, key)),
        ],
        out_specs=[
            pl.BlockSpec((count, BLK, wide), lambda key: (key, 0, 0)),
            whole(heads_here, blocks, DK, wide),
            pl.BlockSpec((1, 2 * count + blocks, BLK), lambda key: (key, 0, 0)),
            whole(heads_here // 2, DK, wide),
            whole(heads_here // 2, DK, wide),
        ],
        out_shape=[
            jax.ShapeDtypeStruct((keys_here * count, BLK, wide), BF16),
            jax.ShapeDtypeStruct((heads_here, blocks, DK, wide), BF16),
            jax.ShapeDtypeStruct((keys_here, 2 * count + blocks, BLK), F32),
            jax.ShapeDtypeStruct((heads_here // 2, DK, wide), BF16),
            jax.ShapeDtypeStruct((heads_here // 2, DK, wide), BF16),
        ],
        scratch_shapes=[
            pltpu.VMEM((count, BLK), F32),
            pltpu.VMEM((count, BLK), F32),
            pltpu.VMEM((blocks, BLK), F32),
            pltpu.VMEM((blocks, DK, BLK), BF16),
            pltpu.VMEM((blocks, BLK, BLK), F32),
            pltpu.VMEM((keys_here * count, DK, wide), BF16),
            pltpu.VMEM((keys_here * count, 1, BLK), F32),
            pltpu.VMEM((heads_here, DK, wide), F32),
        ],
        compiler_params=pltpu.CompilerParams(vmem_limit_bytes=62 * MIB),
        cost_estimate=pl.CostEstimate(
            flops=keys_here * count * 18 * 2 * BLK**3, bytes_accessed=12 * MIB, transcendentals=0
        ),
        name="shard_pass",
    )(me, log_gate, write_rate, starts, key_rows, value_rows)


def local_kernel(per_key, blocks, rows_ref, q_ref, k_ref, wu_ref, zc_ref, out_ref, carry_ref):
    count = per_key * blocks
    cum = rows_ref[0, 0:count, :]
    right = rows_ref[0, count : 2 * count, :]
    reset = rows_ref[0, 2 * count :, :]
    cols = columns_of(jnp.concatenate([cum, reset], axis=0))
    units, inner, masks = [], [], []
    for c in range(blocks):
        span = slice(c * BLK, (c + 1) * BLK)
        query = q_ref[span, :].astype(F32)
        units.append(jnp.sum(query * query, axis=1, keepdims=True) + EPS)
        inner.append(dot_t(q_ref[span, :], k_ref[span, :]))
        masks.append(doc_mask(cols[:, count + c : count + c + 1], reset[c : c + 1, :], False))
    scores = []
    for at in range(count):
        c = at % blocks
        left = cols[:, at : at + 1] - 0.5 * jnp.log(units[c])
        gap = left - right[at : at + 1, :] + masks[c]
        scores.append((inner[c] * jnp.exp(gap)).astype(BF16))
    seen = [dot(scores[at], wu_ref[at]) for at in range(count)]
    for at in range(count):
        c, h = at % blocks, at // blocks
        span = slice(c * BLK, (c + 1) * BLK)
        reset_col = cols[:, count + c : count + c + 1]
        keep = jnp.where(reset_col == 0.0, jnp.exp(cols[:, at : at + 1]), 0.0) * lax.rsqrt(units[c])
        g = (keep * q_ref[span, :].astype(F32) - seen[at][:, :DK]).astype(BF16)
        both = dot(g, zc_ref[h, c])
        out_ref[span, h * DV : (h + 1) * DV] = both[:, :DV] + seen[at][:, DK:]
        carry_ref[span, h * DK : (h + 1) * DK] = both[:, DV:].astype(BF16)


def local_pass(key, rows, queries, key_rows, wu, zc, per_key):
    tokens_here = queries.shape[0]
    blocks = tokens_here // BLK
    count = per_key * blocks
    wide = DK + DV
    return pl.pallas_call(
        functools.partial(local_kernel, per_key, blocks),
        grid=(1,),
        in_specs=[
            pl.BlockSpec((1, 2 * count + blocks, BLK), lambda i: (key, 0, 0)),
            pl.BlockSpec((tokens_here, DK), lambda i: (0, key)),
            pl.BlockSpec((tokens_here, DK), lambda i: (0, key)),
            pl.BlockSpec((count, BLK, wide), lambda i: (key, 0, 0)),
            pl.BlockSpec((per_key, blocks, DK, wide), lambda i: (key, 0, 0, 0)),
        ],
        out_specs=[
            pl.BlockSpec((tokens_here, per_key * DV), lambda i: (0, 0)),
            pl.BlockSpec((tokens_here, per_key * DK), lambda i: (0, 0)),
        ],
        out_shape=[
            jax.ShapeDtypeStruct((tokens_here, per_key * DV), F32),
            jax.ShapeDtypeStruct((tokens_here, per_key * DK), BF16),
        ],
        compiler_params=pltpu.CompilerParams(vmem_limit_bytes=32 * MIB),
        cost_estimate=pl.CostEstimate(
            flops=count * 8 * 2 * BLK**3, bytes_accessed=4 * MIB, transcendentals=0
        ),
        name="local_pass",
    )(rows, queries, key_rows, wu, zc)


def finish_kernel(
    per_key, keys_here, sends, order,
    me_ref, *refs,
):
    half = keys_here * per_key // 2
    odd = lax.rem(me_ref[1], 2) == 1
    outs = refs[:keys_here]
    carries = refs[keys_here : 2 * keys_here]
    own_ref, back_ref, gate_ref, gain_ref, weight_ref, send_ref, keep_ref, normed = refs[2 * keys_here :]
    step = pl.program_id(0)

    @pl.when(step == 0)
    def _():
        for key in range(keys_here):
            for h in range(per_key):
                head = key * per_key + h
                span = slice(h * DV, (h + 1) * DV)
                wide = slice(head * DV, (head + 1) * DV)
                own, back = own_ref[head % half], back_ref[head % half]
                start = jnp.where(odd, own, back) if head >= half else jnp.where(odd, back, own)
                seen = outs[key][:, span] + dot(carries[key][:, span], start)
                spread = jnp.mean(seen * seen, axis=1, keepdims=True)
                gate = gate_ref[:, wide].astype(F32)
                gated = gain_ref[...] * (gate / (1.0 + jnp.exp(-gate)))
                normed[:, wide] = (seen * lax.rsqrt(spread + EPS) * gated).astype(BF16)

    part = dot(normed[...], weight_ref[...]).astype(BF16)

    @pl.when(step < sends)
    def _():
        send_ref[...] = part

    @pl.when(step >= sends)
    def _():
        keep_ref[...] = part


def bit_reversed(size):
    order = [0]
    bit = 1
    while bit < size:
        order = [p for p in order] + [p | bit for p in order]
        bit *= 2
    half = size // 2
    reach = []

    def split(group, bit):
        if len(group) == 1:
            return group
        return split([p for p in group if not p & bit], 2 * bit) + split(
            [p for p in group if p & bit], 2 * bit
        )

    return split(list(range(size)), 1)


def finish_pass(index, rows, me, outs, carries, own, back, out_gate, gain, weight, per_key, groups):
    heads_here = out_gate.shape[1] // DV
    keys_here = len(outs)
    columns = weight.shape[1] // groups
    order = bit_reversed(groups)
    half = groups // 2
    order = order[half:] + order[:half]

    def column_of(step, me_ref):
        place = order[0]
        for at in range(1, groups):
            place = jnp.where(step == at, order[at], place)
        return (0, me_ref[0] ^ place)

    per_head = pl.BlockSpec((rows, per_key * DV), lambda step, me_ref: (index, 0))
    grid_spec = pltpu.PrefetchScalarGridSpec(
        num_scalar_prefetch=1,
        grid=(groups,),
        in_specs=[per_head] * (2 * keys_here)
        + [
            pl.BlockSpec((heads_here // 2, DK, DV), lambda step, me_ref: (0, 0, 0)),
            pl.BlockSpec((heads_here // 2, DK, DV), lambda step, me_ref: (0, 0, 0)),
            pl.BlockSpec((rows, heads_here * DV), lambda step, me_ref: (index, 0)),
            pl.BlockSpec((1, DV), lambda step, me_ref: (0, 0)),
            pl.BlockSpec((weight.shape[0], columns), column_of),
        ],
        out_specs=[
            pl.BlockSpec((rows, columns), lambda step, me_ref: (0, jnp.minimum(step, half - 1))),
            pl.BlockSpec((rows, columns), lambda step, me_ref: (0, jnp.maximum(step - half, 0))),
        ],
        scratch_shapes=[pltpu.VMEM((rows, heads_here * DV), BF16)],
    )
    return pl.pallas_call(
        functools.partial(finish_kernel, per_key, keys_here, half, order),
        grid_spec=grid_spec,
        out_shape=[jax.ShapeDtypeStruct((rows, half * columns), BF16)] * 2,
        compiler_params=pltpu.CompilerParams(vmem_limit_bytes=32 * MIB),
        cost_estimate=pl.CostEstimate(
            flops=2 * rows * weight.shape[0] * weight.shape[1],
            bytes_accessed=8 * MIB,
            transcendentals=0,
        ),
        name="finish_pass",
    )(me, *outs, *carries, own, back, out_gate, gain, weight)


def composed(later, earlier, h):
    return dot(later[h, :, DV:], earlier[h]) + later[h, :, :DV].astype(F32)


def pair_kernel(me_ref, mine_ref, got_ref, both_ref):
    odd = lax.rem(me_ref[0], 2) == 1

    def join(second, first):
        for h in range(both_ref.shape[0]):
            moved = dot(second[h, :, DV:], first[h])
            both_ref[h, :, :DV] = (moved[:, :DV] + second[h, :, :DV].astype(F32)).astype(BF16)
            both_ref[h, :, DV:] = moved[:, DV:].astype(BF16)

    @pl.when(odd)
    def _():
        join(mine_ref, got_ref)

    @pl.when(jnp.logical_not(odd))
    def _():
        join(got_ref, mine_ref)


def step_kernel(later_ref, earlier_ref, out_ref):
    for h in range(out_ref.shape[0]):
        out_ref[h] = composed(later_ref, earlier_ref, h).astype(BF16)


def last_kernel(me_ref, mine_ref, got_ref, before_ref, near_ref, far_ref, own_ref, other_ref):
    odd = lax.rem(me_ref[0], 2) == 1
    third = lax.div(me_ref[0], 2) == 2

    def fill(first, here_ref, then_ref):
        for h in range(own_ref.shape[0]):
            here = composed(before_ref, far_ref, h).astype(BF16)
            here_ref[h] = jnp.where(third, near_ref[h], here)
        for h in range(own_ref.shape[0]):
            then_ref[h] = composed(first, here_ref, h).astype(BF16)

    @pl.when(odd)
    def _():
        fill(got_ref, other_ref, own_ref)

    @pl.when(jnp.logical_not(odd))
    def _():
        fill(mine_ref, own_ref, other_ref)


SMALL = pltpu.CompilerParams(vmem_limit_bytes=8 * MIB)
ONE = pl.BlockSpec(memory_space=pltpu.SMEM)


def plain(array):
    return pl.BlockSpec(array.shape, lambda i: (0,) * array.ndim)


def small_call(kernel, name, outs, me, *arrays):
    heads = arrays[0].shape[0]
    state = jax.ShapeDtypeStruct((heads, DK, DV), BF16)
    scalars = [] if me is None else [me]
    return pl.pallas_call(
        kernel,
        grid=(1,),
        in_specs=[ONE] * len(scalars) + [plain(a) for a in arrays],
        out_specs=[plain(a) for a in outs],
        out_shape=outs,
        compiler_params=SMALL,
        cost_estimate=pl.CostEstimate(
            flops=heads * 4 * DK**3, bytes_accessed=MIB, transcendentals=0
        ),
        name=name,
    )(*scalars, *arrays)


def step_call(later, earlier):
    heads = later.shape[0]
    return pl.pallas_call(
        step_kernel,
        grid=(1,),
        in_specs=[
            pl.BlockSpec((heads, DK, DK + DV), lambda i: (0, 0, 0)),
            pl.BlockSpec((heads, DK, DV), lambda i: (0, 0, 0)),
        ],
        out_specs=pl.BlockSpec((heads, DK, DV), lambda i: (0, 0, 0)),
        out_shape=jax.ShapeDtypeStruct((heads, DK, DV), BF16),
        compiler_params=SMALL,
        cost_estimate=pl.CostEstimate(
            flops=heads * 2 * DK**3, bytes_accessed=MIB, transcendentals=0
        ),
        name="step",
    )(later, earlier)


def route(axis, target):
    size = lax.axis_size(axis)
    return [(i, target(i)) for i in range(size) if target(i) is not None]


def start_states(me, mine, theirs, work):
    size = lax.axis_size("seq")
    half = mine.shape[0]
    state = jax.ShapeDtypeStruct((half, DK, DV), BF16)
    swap = route("seq", lambda i: i ^ 1)
    if size == 8:
        got = work(lax.ppermute(theirs, "seq", swap))
        both, = small_call(
            pair_kernel, "pair", [jax.ShapeDtypeStruct(mine.shape, BF16)], me, mine, got
        )
        before = work(
            lax.ppermute(both, "seq", route("seq", lambda i: i + 2 if i < 6 else None))
        )
        third = step_call(both, before)
        near = lax.ppermute(third, "seq", [(2, 4), (3, 5)])
        far = work(lax.ppermute(third, "seq", [(2, 6), (3, 7)]))
        own, other = small_call(
            last_kernel, "last", [state] * 2, me, mine, got, before, near, far
        )
        return own, work(lax.ppermute(other, "seq", swap))

    onward = route("seq", lambda i: i + 1 if i + 1 < size else None)
    parts = jnp.zeros((half, DK, DV), BF16), jnp.zeros((half, DK, DV), BF16)
    odd = me[0] % 2 == 1

    def hop(step, states):
        ends = [step_call(end, held) for end, held in zip((mine, theirs), states)]
        low, high = jnp.where(odd, ends[1], ends[0]), jnp.where(odd, ends[0], ends[1])
        low, high = lax.ppermute((low, high), "seq", onward)
        return jnp.where(odd, high, low), jnp.where(odd, low, high)

    return lax.fori_loop(0, size - 1, hop, parts)


def local(
    queries, key_rows, value_rows, out_gate, write_rate, log_gate, doc_start, norm_gain, out_weight
):
    tokens_here = queries.shape[0]
    heads_here = value_rows.shape[1] // DV
    keys_here = key_rows.shape[1] // DK
    per_key = heads_here // keys_here
    groups = lax.axis_size("head")
    starts = doc_start.reshape(tokens_here // BLK, BLK)
    seq_me = lax.axis_index("seq").reshape(1).astype(jnp.int32)
    head_me = lax.axis_index("head").reshape(1).astype(jnp.int32)
    wu, zc, rows, mine, theirs = shard_pass(
        seq_me, log_gate, write_rate, starts, key_rows, value_rows, per_key
    )
    outs, carries = [], []

    def work(coming):
        key = len(outs)
        if key == keys_here:
            return coming
        out, carry = local_pass(key, rows, queries, key_rows, wu, zc, per_key)
        coming, out, carry = lax.optimization_barrier((coming, out, carry))
        outs.append(out)
        carries.append(carry)
        return coming

    own, back = start_states(seq_me, mine, theirs, work)
    while len(outs) < keys_here:
        back = work(back)

    me = jnp.concatenate([head_me, seq_me])
    chunks = 4
    rows_each = tokens_here // chunks
    gain = norm_gain.reshape(1, DV)

    def project(index, ready):
        nonlocal back
        if ready is not None:
            back, ready = lax.optimization_barrier((back, ready))
        pair = finish_pass(
            index, rows_each, me, outs, carries, own, back, out_gate, gain, out_weight, per_key, groups
        )
        return ready, pair

    pieces = []
    ready, (send, keep) = project(0, None)
    for index in range(chunks):
        following = None
        bit = 1
        while bit < groups:
            got = lax.ppermute(send, "head", route("head", lambda i: i ^ bit))
            if bit == 1 and index + 1 < chunks:
                following = project(index + 1, send)[1]
                got, held = lax.optimization_barrier((got, following[0]))
                following = (held, following[1])
            total = keep.astype(F32) + got.astype(F32)
            bit *= 2
            if bit < groups:
                width = total.shape[1] // 2
                keep = total[:, :width]
                send = total[:, width:].astype(BF16)
            else:
                keep = total
        pieces.append(keep.astype(BF16))
        if following is not None:
            send, keep = following
    return jnp.concatenate(pieces, axis=0)


def solution(mesh):
    placed = (
        P("seq", "head"),
        P("seq", "head"),
        P("seq", "head"),
        P("seq", "head"),
        P("head", "seq"),
        P("head", "seq"),
        P("seq"),
        P(),
        P("head", None),
    )
    return jax.shard_map(
        local, mesh=mesh, in_specs=placed, out_specs=P("seq", "head"), check_vma=False
    )
```

```python
import functools

import jax
import jax.numpy as jnp
from jax import lax
from jax.experimental import pallas as pl
from jax.experimental.pallas import tpu as pltpu
from jax.sharding import PartitionSpec as P

DK = 128
DV = 128
BLK = 128
SUB = 16
EPS = 1e-06
FAR = -1e30
F32 = jnp.float32
BF16 = jnp.bfloat16
MIB = 1024 * 1024


def dot(a, b):
    return jnp.dot(a, b, preferred_element_type=F32)


def dot_t(a, b):
    return lax.dot_general(a, b, (((1,), (1,)), ((), ())), preferred_element_type=F32)


def running_sum(values):
    lane = lax.broadcasted_iota(jnp.int32, values.shape, 1)
    step = 1
    while step < BLK:
        values = values + jnp.where(lane >= step, pltpu.roll(values, step, 1), 0.0)
        step *= 2
    return values


def columns_of(rows):
    pad = BLK - rows.shape[0]
    return jnp.transpose(jnp.concatenate([rows, jnp.zeros((pad, BLK), F32)], axis=0))


def doc_mask(reset_col, reset_row, strict):
    i = lax.broadcasted_iota(jnp.int32, (BLK, BLK), 0)
    j = lax.broadcasted_iota(jnp.int32, (BLK, BLK), 1)
    below = (i > j) if strict else (i >= j)
    return jnp.where(below & (reset_col == reset_row), 0.0, FAR)


def small_inverses(lower, count):
    lane = lax.broadcasted_iota(jnp.int32, (SUB, BLK), 1)
    packed = []
    for m in lower:
        kept = m[:SUB]
        for b in range(1, BLK // SUB):
            kept = jnp.where(lane // SUB == b, m[b * SUB : (b + 1) * SUB], kept)
        packed.append(kept.astype(BF16))
    packed = jnp.concatenate(packed, axis=0)
    i = lax.broadcasted_iota(jnp.int32, (BLK, BLK), 0)
    j = lax.broadcasted_iota(jnp.int32, (BLK, BLK), 1)
    same = i // SUB == j // SUB
    place = lax.broadcasted_iota(jnp.int32, (count, SUB, BLK), 1)
    lanes = lax.broadcasted_iota(jnp.int32, (count, SUB, BLK), 2)
    found = jnp.where(place == lanes % SUB, 1.0, 0.0)
    for m in range(0, SUB, 2):
        spread = [jnp.where(same & (i % SUB == m + d), 1.0, 0.0).astype(BF16) for d in range(2)]
        pair = dot(packed, jnp.concatenate(spread, axis=1)).reshape(count, SUB, 2 * BLK)
        for d in range(2):
            if m + d < SUB - 1:
                found = found - pair[:, :, d * BLK : (d + 1) * BLK] * found[:, m + d : m + d + 1, :]
    return found.astype(BF16)


def odd_rows(matrix, size):
    return jnp.concatenate(
        [matrix[p : p + size] for p in range(size, BLK, 2 * size)], axis=0
    )


def with_odd_rows(matrix, rows, size):
    parts = []
    for p in range(0, BLK, 2 * size):
        parts.append(matrix[p : p + size])
        parts.append(rows[p // 2 : p // 2 + size])
    return jnp.concatenate(parts, axis=0)


def shard_kernel(
    first, per_key, blocks, keys,
    me_ref, log_ref, rate_ref, start_ref, k_ref, v_ref,
    wu_ref, zc_ref, rows_ref, mine_ref, theirs_ref,
    logs, rates, norms, kt, db, keep, state,
):
    heads = keys * per_key
    count = heads * blocks
    for h in range(heads):
        head = first * per_key + h
        for c in range(blocks):
            at = h * blocks + c
            span = slice(c * BLK, (c + 1) * BLK)
            logs[at : at + 1, :] = log_ref[head : head + 1, span]
            rates[at : at + 1, :] = rate_ref[head : head + 1, span]

    starts = start_ref[...].astype(F32)
    sums = running_sum(jnp.concatenate([logs[...], starts], axis=0))
    cum, reset = sums[:count], sums[count:]
    inner = []
    for key in range(keys):
        for c in range(blocks):
            rows = k_ref[c * BLK : (c + 1) * BLK, key * DK : (key + 1) * DK]
            flipped = jnp.transpose(rows.astype(F32))
            turned = flipped.astype(BF16)
            kt[key * blocks + c] = turned
            norms[key * blocks + c : key * blocks + c + 1, :] = jnp.sum(
                flipped * flipped, axis=0, keepdims=True
            )
            inner.append(dot(rows, turned))
    reset_cols = columns_of(reset)
    masks = [doc_mask(reset_cols[:, c : c + 1], reset[c : c + 1, :], True) for c in range(blocks)]

    squares = norms[...] + EPS
    squares = jnp.concatenate(
        [squares[(h // per_key) * blocks : (h // per_key + 1) * blocks] for h in range(heads)], axis=0
    )
    scale = lax.rsqrt(squares)
    log_scale = -0.5 * jnp.log(squares)
    resets = jnp.concatenate([reset] * heads, axis=0)
    rate = rates[...]
    last = cum[:, BLK - 1 :]
    last_reset = resets[:, BLK - 1 :]
    left_cols = columns_of(cum + jnp.log(rate) + log_scale)
    right = cum - log_scale
    head_keep = jnp.where(resets == 0.0, jnp.exp(cum), 0.0)
    tail = jnp.where(resets == last_reset, jnp.exp(last - cum), 0.0) * scale
    erase_row = rate * head_keep * scale
    keep[...] = jnp.broadcast_to(jnp.where(last_reset == 0.0, jnp.exp(last), 0.0), (count, BLK))
    rows_ref[0:count, :] = cum
    rows_ref[count : 2 * count, :] = right
    rows_ref[2 * count :, :] = reset

    lower = []
    for at in range(count):
        c = at % blocks
        gap = left_cols[:, at : at + 1] - right[at : at + 1, :] + masks[c]
        lower.append(inner[at // (per_key * blocks) * blocks + c] * jnp.exp(gap))
    packed = small_inverses(lower, count)
    lower = [m.astype(BF16) for m in lower]
    lane = lax.broadcasted_iota(jnp.int32, (SUB, BLK), 1)
    zero = jnp.zeros((SUB, BLK), BF16)
    ones = [jnp.where(lane // SUB == b, 1.0, 0.0).astype(BF16) for b in range(BLK // SUB)]
    inverse = [
        jnp.concatenate([packed[at] * ones[b] for b in range(BLK // SUB)], axis=0)
        for at in range(count)
    ]
    size = SUB
    while size < BLK:
        i = lax.broadcasted_iota(jnp.int32, (BLK // 2, BLK), 0)
        j = lax.broadcasted_iota(jnp.int32, (BLK // 2, BLK), 1)
        reach = jnp.where(j // size == 2 * (i // size), 1.0, 0.0).astype(BF16)
        odd = [odd_rows(t, size) for t in inverse]
        half = [dot(o, m).astype(BF16) * reach for o, m in zip(odd, lower)]
        fresh = [o - dot(f, t).astype(BF16) for o, f, t in zip(odd, half, inverse)]
        inverse = [with_odd_rows(t, f, size) for t, f in zip(inverse, fresh)]
        size *= 2
    for at in range(count):
        c, h = at % blocks, at // blocks
        key = h // per_key
        span = slice(c * BLK, (c + 1) * BLK)
        t = inverse[at].astype(F32)
        erase = dot(
            (t * erase_row[at : at + 1, :]).astype(BF16), k_ref[span, key * DK : (key + 1) * DK]
        )
        write = dot((t * rate[at : at + 1, :]).astype(BF16), v_ref[span, h * DV : (h + 1) * DV])
        wu_ref[at, :, :DK] = erase.astype(BF16)
        wu_ref[at, :, DK:] = write.astype(BF16)
    for at in range(count):
        c, key = at % blocks, at // (per_key * blocks)
        tailed = (kt[key * blocks + c].astype(F32) * tail[at : at + 1, :]).astype(BF16)
        db[at] = dot(tailed, wu_ref[at]).astype(BF16)

    i = lax.broadcasted_iota(jnp.int32, (DK, DK), 0)
    j = lax.broadcasted_iota(jnp.int32, (DK, DK), 1)
    for h in range(heads):
        state[h, :, :DV] = jnp.zeros((DK, DV), F32)
        state[h, :, DV:] = jnp.where(i == j, 1.0, 0.0)
    for c in range(blocks):
        for h in range(heads):
            now = state[h]
            low = now.astype(BF16)
            at = h * blocks + c
            zc_ref[at] = low
            moved = dot(db[at, :, :DK], low)
            g = keep[at : at + 1, :]
            state[h, :, :DV] = g * now[:, :DV] - moved[:, :DV] + db[at, :, DK:].astype(F32)
            state[h, :, DV:] = g * now[:, DV:] - moved[:, DV:]
    half = heads // 2
    odd = lax.rem(me_ref[0], 2) == 1
    for h in range(heads):
        ends = state[h].astype(BF16)
        ours = odd if h >= half else jnp.logical_not(odd)

        @pl.when(ours)
        def _():
            mine_ref[h % half] = ends

        @pl.when(jnp.logical_not(ours))
        def _():
            theirs_ref[h % half] = ends


def vmem(shape, dtype):
    return pltpu.VMEM(shape, dtype)


def in_hbm(array):
    return pltpu.with_memory_space_constraint(array, pltpu.HBM)


def in_vmem():
    return pl.BlockSpec(memory_space=pltpu.VMEM)


def shard_pass(group, groups, me, log_gate, write_rate, starts, key_rows, value_rows, per_key):
    tokens_here = key_rows.shape[0]
    keys = key_rows.shape[1] // DK // groups
    heads = keys * per_key
    heads_here = heads * groups
    blocks = tokens_here // BLK
    count = heads * blocks
    wide = DK + DV
    whole = lambda *shape: pl.BlockSpec(shape, lambda i: (0,) * len(shape))
    return pl.pallas_call(
        functools.partial(shard_kernel, group * keys, per_key, blocks, keys),
        grid=(1,),
        in_specs=[
            pl.BlockSpec(memory_space=pltpu.SMEM),
            whole(heads_here, tokens_here),
            whole(heads_here, tokens_here),
            whole(blocks, BLK),
            pl.BlockSpec((tokens_here, keys * DK), lambda i: (0, group)),
            pl.BlockSpec((tokens_here, heads * DV), lambda i: (0, group)),
        ],
        out_specs=[in_vmem()] * 5,
        out_shape=[
            vmem((count, BLK, wide), BF16),
            vmem((count, DK, wide), BF16),
            vmem((2 * count + blocks, BLK), F32),
            vmem((heads // 2, DK, wide), BF16),
            vmem((heads // 2, DK, wide), BF16),
        ],
        scratch_shapes=[
            pltpu.VMEM((count, BLK), F32),
            pltpu.VMEM((count, BLK), F32),
            pltpu.VMEM((keys * blocks, BLK), F32),
            pltpu.VMEM((keys * blocks, DK, BLK), BF16),
            pltpu.VMEM((count, DK, wide), BF16),
            pltpu.VMEM((count, BLK), F32),
            pltpu.VMEM((heads, DK, wide), F32),
        ],
        compiler_params=pltpu.CompilerParams(vmem_limit_bytes=24 * MIB),
        cost_estimate=pl.CostEstimate(
            flops=count * 18 * 2 * BLK**3, bytes_accessed=4 * MIB, transcendentals=0
        ),
        name="shard_pass",
    )(me, *(in_hbm(a) for a in (log_gate, write_rate, starts, key_rows, value_rows)))


def local_kernel(
    per_key, blocks, at_key, rows_ref, q_ref, k_ref, gate_ref, gain_ref, wu_ref, zc_ref,
    out_ref, carry_ref, gated_ref,
):
    count = per_key * blocks
    total = (rows_ref.shape[0] - blocks) // 2
    base = at_key * count
    cum = rows_ref[base : base + count, :]
    right = rows_ref[total + base : total + base + count, :]
    reset = rows_ref[2 * total :, :]
    cols = columns_of(jnp.concatenate([cum, reset], axis=0))
    units, inner, masks = [], [], []
    for c in range(blocks):
        span = slice(c * BLK, (c + 1) * BLK)
        query = q_ref[span, :].astype(F32)
        units.append(jnp.sum(query * query, axis=1, keepdims=True) + EPS)
        inner.append(dot_t(q_ref[span, :], k_ref[span, :]))
        masks.append(doc_mask(cols[:, count + c : count + c + 1], reset[c : c + 1, :], False))
    scores = []
    for at in range(count):
        c = at % blocks
        left = cols[:, at : at + 1] - 0.5 * jnp.log(units[c])
        gap = left - right[at : at + 1, :] + masks[c]
        scores.append((inner[c] * jnp.exp(gap)).astype(BF16))
    seen = [dot(scores[at], wu_ref[base + at]) for at in range(count)]
    for at in range(count):
        c, h = at % blocks, at // blocks
        span = slice(c * BLK, (c + 1) * BLK)
        wide = slice(h * DV, (h + 1) * DV)
        reset_col = cols[:, count + c : count + c + 1]
        keep = jnp.where(reset_col == 0.0, jnp.exp(cols[:, at : at + 1]), 0.0) * lax.rsqrt(units[c])
        g = (keep * q_ref[span, :].astype(F32) - seen[at][:, :DK]).astype(BF16)
        both = dot(g, zc_ref[base + at])
        out_ref[span, wide] = both[:, :DV] + seen[at][:, DK:]
        carry_ref[span, wide] = both[:, DV:].astype(BF16)
        gate = gate_ref[span, wide].astype(F32)
        gated_ref[span, wide] = gain_ref[...] * (gate / (1.0 + jnp.exp(-gate)))


def local_pass(key, at_key, rows, queries, key_rows, out_gate, gain, wu, zc, per_key):
    tokens_here = queries.shape[0]
    blocks = tokens_here // BLK
    count = per_key * blocks
    wide = per_key * DV
    return pl.pallas_call(
        functools.partial(local_kernel, per_key, blocks, at_key),
        grid=(1,),
        in_specs=[
            in_vmem(),
            pl.BlockSpec((tokens_here, DK), lambda i: (0, key)),
            pl.BlockSpec((tokens_here, DK), lambda i: (0, key)),
            pl.BlockSpec((tokens_here, wide), lambda i: (0, key)),
            pl.BlockSpec((1, DV), lambda i: (0, 0)),
            in_vmem(),
            in_vmem(),
        ],
        out_specs=[in_vmem()] * 3,
        out_shape=[
            vmem((tokens_here, wide), F32),
            vmem((tokens_here, wide), BF16),
            vmem((tokens_here, wide), F32),
        ],
        compiler_params=pltpu.CompilerParams(vmem_limit_bytes=16 * MIB),
        cost_estimate=pl.CostEstimate(
            flops=count * 8 * 2 * BLK**3, bytes_accessed=4 * MIB, transcendentals=0
        ),
        name="local_pass",
    )(rows, queries, key_rows, out_gate, gain, wu, zc)


def finish_kernel(row, per_key, keys_here, group_heads, order, me_ref, *refs):
    outs = refs[:keys_here]
    carries = refs[keys_here : 2 * keys_here]
    gates = refs[2 * keys_here : 3 * keys_here]
    refs = refs[3 * keys_here :]
    groups = keys_here * per_key // group_heads
    starts = refs[: 2 * groups]
    weight_ref, send_ref, keep_ref = refs[2 * groups :]
    rows = slice(row, row + send_ref.shape[0])
    half = group_heads // 2
    odd = lax.rem(me_ref[0], 2) == 1
    parts = []
    for head in range(keys_here * per_key):
        key, h = head // per_key, head % per_key
        span = slice(h * DV, (h + 1) * DV)
        own_ref, back_ref = starts[2 * (head // group_heads) : 2 * (head // group_heads) + 2]
        own, back = own_ref[head % half], back_ref[head % half]
        start = jnp.where(odd, own, back) if head % group_heads >= half else jnp.where(odd, back, own)
        seen = outs[key][rows, span] + dot(carries[key][rows, span], start)
        spread = jnp.mean(seen * seen, axis=1, keepdims=True)
        parts.append((seen * lax.rsqrt(spread + EPS) * gates[key][rows, span]).astype(BF16))
    normed = jnp.concatenate(parts, axis=1)
    columns = weight_ref.shape[1] // len(order)
    sends = len(order) // 2
    for at, place in enumerate(order):
        first = pl.multiple_of((me_ref[1] ^ place) * columns, columns)
        part = dot(normed, weight_ref[:, pl.ds(first, columns)]).astype(BF16)
        to, slot = (send_ref, at - sends) if at >= sends else (keep_ref, at)
        to[:, slot * columns : (slot + 1) * columns] = part


def halving_order(size):
    def split(group, bit):
        if len(group) == 1:
            return group
        kept = [p for p in group if not p & bit]
        return split(kept, 2 * bit) + split([p for p in group if p & bit], 2 * bit)

    return split(list(range(size)), 1)


def finish_pass(row, rows, me, outs, carries, gates, starts, weight, per_key, group_heads, devices):
    keys_here = len(outs)
    half = weight.shape[1] // 2
    return pl.pallas_call(
        functools.partial(
            finish_kernel, row, per_key, keys_here, group_heads, halving_order(devices)
        ),
        grid=(1,),
        in_specs=[pl.BlockSpec(memory_space=pltpu.SMEM)]
        + [in_vmem()] * (3 * keys_here + len(starts) + 1),
        out_specs=[in_vmem()] * 2,
        out_shape=[vmem((rows, half), BF16)] * 2,
        compiler_params=pltpu.CompilerParams(vmem_limit_bytes=16 * MIB),
        cost_estimate=pl.CostEstimate(
            flops=2 * rows * weight.shape[0] * weight.shape[1],
            bytes_accessed=8 * MIB,
            transcendentals=0,
        ),
        name="finish_pass",
    )(me, *outs, *carries, *gates, *starts, weight)


def composed(later, earlier, h):
    return dot(later[h, :, DV:], earlier[h]) + later[h, :, :DV].astype(F32)


def pair_kernel(me_ref, mine_ref, got_ref, both_ref):
    odd = lax.rem(me_ref[0], 2) == 1

    def join(second, first):
        for h in range(both_ref.shape[0]):
            moved = dot(second[h, :, DV:], first[h])
            both_ref[h, :, :DV] = (moved[:, :DV] + second[h, :, :DV].astype(F32)).astype(BF16)
            both_ref[h, :, DV:] = moved[:, DV:].astype(BF16)

    @pl.when(odd)
    def _():
        join(mine_ref, got_ref)

    @pl.when(jnp.logical_not(odd))
    def _():
        join(got_ref, mine_ref)


def step_kernel(later_ref, earlier_ref, out_ref):
    for h in range(out_ref.shape[0]):
        out_ref[h] = composed(later_ref, earlier_ref, h).astype(BF16)


def last_kernel(me_ref, mine_ref, got_ref, before_ref, near_ref, far_ref, own_ref, other_ref):
    odd = lax.rem(me_ref[0], 2) == 1
    third = lax.div(me_ref[0], 2) == 2

    def fill(first, here_ref, then_ref):
        for h in range(own_ref.shape[0]):
            here = composed(before_ref, far_ref, h).astype(BF16)
            here_ref[h] = jnp.where(third, near_ref[h], here)
        for h in range(own_ref.shape[0]):
            then_ref[h] = composed(first, here_ref, h).astype(BF16)

    @pl.when(odd)
    def _():
        fill(got_ref, other_ref, own_ref)

    @pl.when(jnp.logical_not(odd))
    def _():
        fill(mine_ref, own_ref, other_ref)


SMALL = pltpu.CompilerParams(vmem_limit_bytes=8 * MIB)
ONE = pl.BlockSpec(memory_space=pltpu.SMEM)


def plain(array):
    return pl.BlockSpec(array.shape, lambda i: (0,) * array.ndim)


def small_call(kernel, name, outs, me, *arrays):
    heads = arrays[0].shape[0]
    state = jax.ShapeDtypeStruct((heads, DK, DV), BF16)
    scalars = [] if me is None else [me]
    return pl.pallas_call(
        kernel,
        grid=(1,),
        in_specs=[ONE] * len(scalars) + [plain(a) for a in arrays],
        out_specs=[plain(a) for a in outs],
        out_shape=outs,
        compiler_params=SMALL,
        cost_estimate=pl.CostEstimate(
            flops=heads * 4 * DK**3, bytes_accessed=MIB, transcendentals=0
        ),
        name=name,
    )(*scalars, *arrays)


def step_call(later, earlier):
    heads = later.shape[0]
    return pl.pallas_call(
        step_kernel,
        grid=(1,),
        in_specs=[
            pl.BlockSpec((heads, DK, DK + DV), lambda i: (0, 0, 0)),
            pl.BlockSpec((heads, DK, DV), lambda i: (0, 0, 0)),
        ],
        out_specs=pl.BlockSpec((heads, DK, DV), lambda i: (0, 0, 0)),
        out_shape=jax.ShapeDtypeStruct((heads, DK, DV), BF16),
        compiler_params=SMALL,
        cost_estimate=pl.CostEstimate(
            flops=heads * 2 * DK**3, bytes_accessed=MIB, transcendentals=0
        ),
        name="step",
    )(later, earlier)


def route(axis, target):
    size = lax.axis_size(axis)
    return [(i, target(i)) for i in range(size) if target(i) is not None]


def start_states(me, mine, theirs, work):
    size = lax.axis_size("seq")
    half = mine.shape[0]
    state = jax.ShapeDtypeStruct((half, DK, DV), BF16)
    swap = route("seq", lambda i: i ^ 1)
    if size == 8:
        got = work(lax.ppermute(theirs, "seq", swap))
        both, = small_call(
            pair_kernel, "pair", [jax.ShapeDtypeStruct(mine.shape, BF16)], me, mine, got
        )
        before = work(
            lax.ppermute(both, "seq", route("seq", lambda i: i + 2 if i < 6 else None))
        )
        third = step_call(both, before)
        near = lax.ppermute(third, "seq", [(2, 4), (3, 5)])
        far = work(lax.ppermute(third, "seq", [(2, 6), (3, 7)]))
        own, other = small_call(
            last_kernel, "last", [state] * 2, me, mine, got, before, near, far
        )
        return own, work(lax.ppermute(other, "seq", swap))

    onward = route("seq", lambda i: i + 1 if i + 1 < size else None)
    parts = jnp.zeros((half, DK, DV), BF16), jnp.zeros((half, DK, DV), BF16)
    odd = me[0] % 2 == 1

    def hop(step, states):
        ends = [step_call(end, held) for end, held in zip((mine, theirs), states)]
        low, high = jnp.where(odd, ends[1], ends[0]), jnp.where(odd, ends[0], ends[1])
        low, high = lax.ppermute((low, high), "seq", onward)
        return jnp.where(odd, high, low), jnp.where(odd, low, high)

    return lax.fori_loop(0, size - 1, hop, parts)


def local(
    queries, key_rows, value_rows, out_gate, write_rate, log_gate, doc_start, norm_gain, out_weight
):
    tokens_here = queries.shape[0]
    heads_here = value_rows.shape[1] // DV
    keys_here = key_rows.shape[1] // DK
    per_key = heads_here // keys_here
    devices = lax.axis_size("head")
    starts = doc_start.reshape(tokens_here // BLK, BLK)
    me = jnp.stack([lax.axis_index("seq"), lax.axis_index("head")]).astype(jnp.int32)
    gain = norm_gain.reshape(1, DV)
    groups = 1
    keys = keys_here // groups
    outs, carries, gates, states = [], [], [], []
    for group in range(groups):
        wu, zc, rows, mine, theirs = shard_pass(
            group, groups, me, log_gate, write_rate, starts, key_rows, value_rows, per_key
        )

        def work(coming):
            key = len(outs)
            if key == (group + 1) * keys:
                return coming
            out, carry, gate = local_pass(
                key, key - group * keys, rows, queries, key_rows, out_gate, gain, wu, zc, per_key
            )
            coming, out, carry, gate = lax.optimization_barrier((coming, out, carry, gate))
            outs.append(out)
            carries.append(carry)
            gates.append(gate)
            return coming

        own, back = start_states(me, mine, theirs, work)
        while len(outs) < (group + 1) * keys:
            back = work(back)
        states += [own, back]

    weight = pltpu.with_memory_space_constraint(out_weight, pltpu.VMEM)

    def project(row, rows, ready):
        if ready is not None:
            states[-1], ready = lax.optimization_barrier((states[-1], ready))
        pair = finish_pass(
            row, rows, me, outs, carries, gates, states, weight, per_key, keys * per_key, devices
        )
        return ready, pair

    sizes = [tokens_here // 8, tokens_here // 4, tokens_here // 4, tokens_here // 4, tokens_here // 8]
    places = [sum(sizes[:index]) for index in range(len(sizes))]
    mixed = jnp.zeros((tokens_here, out_weight.shape[1] // devices), BF16)
    send, keep = project(places[0], sizes[0], None)[1]
    for index, place in enumerate(places):
        following = None
        bit = 1
        while bit < devices:
            got = lax.ppermute(send, "head", route("head", lambda i: i ^ bit))
            if bit == 1 and index + 1 < len(sizes):
                following = project(places[index + 1], sizes[index + 1], send)[1]
                got, *following = lax.optimization_barrier((got, *following))
            total = keep.astype(F32) + got.astype(F32)
            bit *= 2
            if bit < devices:
                width = total.shape[1] // 2
                keep = total[:, :width]
                send = total[:, width:].astype(BF16)
                if bit == 2 and following is not None:
                    states[-1], send = lax.optimization_barrier((states[-1], send))
            else:
                keep = total
        mixed = lax.dynamic_update_slice(mixed, keep.astype(BF16), (place, 0))
        if following is not None:
            send, keep = following
    return mixed


def solution(mesh):
    placed = (
        P("seq", "head"),
        P("seq", "head"),
        P("seq", "head"),
        P("seq", "head"),
        P("head", "seq"),
        P("head", "seq"),
        P("seq"),
        P(),
        P("head", None),
    )
    return jax.shard_map(
        local, mesh=mesh, in_specs=placed, out_specs=P("seq", "head"), check_vma=False
    )
```

```python
import functools

import jax
import jax.numpy as jnp
from jax import lax
from jax.experimental import pallas as pl
from jax.experimental.pallas import tpu as pltpu
from jax.sharding import PartitionSpec as P

DK = 128
DV = 128
BLK = 128
SUB = 16
EPS = 1e-06
FAR = -1e30
F32 = jnp.float32
BF16 = jnp.bfloat16
MIB = 1024 * 1024


def dot(a, b):
    return jnp.dot(a, b, preferred_element_type=F32)


def dot_t(a, b):
    return lax.dot_general(a, b, (((1,), (1,)), ((), ())), preferred_element_type=F32)


def running_sum(values):
    lane = lax.broadcasted_iota(jnp.int32, values.shape, 1)
    step = 1
    while step < BLK:
        values = values + jnp.where(lane >= step, pltpu.roll(values, step, 1), 0.0)
        step *= 2
    return values


def columns_of(rows):
    pad = BLK - rows.shape[0]
    return jnp.transpose(jnp.concatenate([rows, jnp.zeros((pad, BLK), F32)], axis=0))


def doc_mask(reset_col, reset_row, strict):
    i = lax.broadcasted_iota(jnp.int32, (BLK, BLK), 0)
    j = lax.broadcasted_iota(jnp.int32, (BLK, BLK), 1)
    below = (i > j) if strict else (i >= j)
    return jnp.where(below & (reset_col == reset_row), 0.0, FAR)


def place_of(part, parts):
    if parts == 1:
        return 0
    odd = lax.rem(lax.axis_index("seq"), 2)
    return odd if part == 1 else 1 - odd


def small_inverses(lower, count):
    lane = lax.broadcasted_iota(jnp.int32, (SUB, BLK), 1)
    packed = []
    for m in lower:
        kept = m[:SUB]
        for b in range(1, BLK // SUB):
            kept = jnp.where(lane // SUB == b, m[b * SUB : (b + 1) * SUB], kept)
        packed.append(kept.astype(BF16))
    packed = jnp.concatenate(packed, axis=0)
    i = lax.broadcasted_iota(jnp.int32, (BLK, BLK), 0)
    j = lax.broadcasted_iota(jnp.int32, (BLK, BLK), 1)
    same = i // SUB == j // SUB
    place = lax.broadcasted_iota(jnp.int32, (count, SUB, BLK), 1)
    lanes = lax.broadcasted_iota(jnp.int32, (count, SUB, BLK), 2)
    found = jnp.where(place == lanes % SUB, 1.0, 0.0)
    for m in range(0, SUB, 2):
        spread = [jnp.where(same & (i % SUB == m + d), 1.0, 0.0).astype(BF16) for d in range(2)]
        pair = dot(packed, jnp.concatenate(spread, axis=1)).reshape(count, SUB, 2 * BLK)
        for d in range(2):
            if m + d < SUB - 1:
                found = found - pair[:, :, d * BLK : (d + 1) * BLK] * found[:, m + d : m + d + 1, :]
    return found.astype(BF16)


def odd_rows(matrix, size):
    return jnp.concatenate(
        [matrix[p : p + size] for p in range(size, BLK, 2 * size)], axis=0
    )


def with_odd_rows(matrix, rows, size):
    parts = []
    for p in range(0, BLK, 2 * size):
        parts.append(matrix[p : p + size])
        parts.append(rows[p // 2 : p // 2 + size])
    return jnp.concatenate(parts, axis=0)


def shard_kernel(
    part, parts, per_key, blocks, keys, *refs
):
    if part == 0:
        log_in, rate_in, start_in, k_in, v_in = refs[:5]
        wu_ref, zc_ref, rows_ref, end_ref, log_ref, rate_ref, start_ref, k_ref, v_ref = refs[5:14]
    else:
        log_ref, rate_ref, start_ref, k_ref, v_ref, wu_ref, zc_ref, rows_ref, end_ref = refs[:9]
    logs, rates, norms, kt, db, keep, state = refs[len(refs) - 7 :] if part else refs[14:21]
    mine = place_of(part, parts)
    small_copies, k_copies, v_copies = [], [], []
    if part == 0:
        small_sems, k_sems, v_sems = refs[21:]
        for at, (ref, here) in enumerate(
            ((log_in, log_ref), (rate_in, rate_ref), (start_in, start_ref))
        ):
            small_copies.append(pltpu.make_async_copy(ref, here, small_sems.at[at]))
        for copies, ref, here, sems in (
            (k_copies, k_in, k_ref, k_sems),
            (v_copies, v_in, v_ref, v_sems),
        ):
            for c in range(blocks):
                span = slice(c * BLK, (c + 1) * BLK)
                copies.append(pltpu.make_async_copy(ref.at[span], here.at[span], sems.at[c]))
        for copy in small_copies + k_copies + v_copies:
            copy.start()
        for copy in small_copies:
            copy.wait()
    key_lanes = lambda key: pl.ds(pl.multiple_of((mine * keys + key) * DK, DK), DK)
    head_lanes = lambda h: pl.ds(pl.multiple_of((mine * keys * per_key + h) * DV, DV), DV)
    heads = keys * per_key
    count = heads * blocks
    for place in range(parts):

        @pl.when(mine == place)
        def _():
            for h in range(heads):
                head = place * heads + h
                for c in range(blocks):
                    at = h * blocks + c
                    span = slice(c * BLK, (c + 1) * BLK)
                    logs[at : at + 1, :] = log_ref[head : head + 1, span]
                    rates[at : at + 1, :] = rate_ref[head : head + 1, span]

    starts = start_ref[...].astype(F32)
    sums = running_sum(jnp.concatenate([logs[...], starts], axis=0))
    cum, reset = sums[:count], sums[count:]
    inner = []
    for copy in k_copies:
        copy.wait()
    for key in range(keys):
        for c in range(blocks):
            rows = k_ref[c * BLK : (c + 1) * BLK, key_lanes(key)]
            flipped = jnp.transpose(rows.astype(F32))
            turned = flipped.astype(BF16)
            kt[key * blocks + c] = turned
            norms[key * blocks + c : key * blocks + c + 1, :] = jnp.sum(
                flipped * flipped, axis=0, keepdims=True
            )
            inner.append(dot(rows, turned))
    reset_cols = columns_of(reset)
    masks = [doc_mask(reset_cols[:, c : c + 1], reset[c : c + 1, :], True) for c in range(blocks)]

    squares = norms[...] + EPS
    squares = jnp.concatenate(
        [squares[(h // per_key) * blocks : (h // per_key + 1) * blocks] for h in range(heads)], axis=0
    )
    scale = lax.rsqrt(squares)
    log_scale = -0.5 * jnp.log(squares)
    resets = jnp.concatenate([reset] * heads, axis=0)
    rate = rates[...]
    last = cum[:, BLK - 1 :]
    last_reset = resets[:, BLK - 1 :]
    left_cols = columns_of(cum + jnp.log(rate) + log_scale)
    right = cum - log_scale
    head_keep = jnp.where(resets == 0.0, jnp.exp(cum), 0.0)
    tail = jnp.where(resets == last_reset, jnp.exp(last - cum), 0.0) * scale
    erase_row = rate * head_keep * scale
    keep[...] = jnp.broadcast_to(jnp.where(last_reset == 0.0, jnp.exp(last), 0.0), (count, BLK))
    rows_ref[0:count, :] = cum
    rows_ref[count : 2 * count, :] = right
    rows_ref[2 * count :, :] = reset

    lower = []
    for at in range(count):
        c = at % blocks
        gap = left_cols[:, at : at + 1] - right[at : at + 1, :] + masks[c]
        lower.append(inner[at // (per_key * blocks) * blocks + c] * jnp.exp(gap))
    packed = small_inverses(lower, count)
    lower = [m.astype(BF16) for m in lower]
    lane = lax.broadcasted_iota(jnp.int32, (SUB, BLK), 1)
    zero = jnp.zeros((SUB, BLK), BF16)
    ones = [jnp.where(lane // SUB == b, 1.0, 0.0).astype(BF16) for b in range(BLK // SUB)]
    inverse = [
        jnp.concatenate([packed[at] * ones[b] for b in range(BLK // SUB)], axis=0)
        for at in range(count)
    ]
    size = SUB
    while size < BLK:
        i = lax.broadcasted_iota(jnp.int32, (BLK // 2, BLK), 0)
        j = lax.broadcasted_iota(jnp.int32, (BLK // 2, BLK), 1)
        reach = jnp.where(j // size == 2 * (i // size), 1.0, 0.0).astype(BF16)
        odd = [odd_rows(t, size) for t in inverse]
        half = [dot(o, m).astype(BF16) * reach for o, m in zip(odd, lower)]
        fresh = [o - dot(f, t).astype(BF16) for o, f, t in zip(odd, half, inverse)]
        inverse = [with_odd_rows(t, f, size) for t, f in zip(inverse, fresh)]
        size *= 2
    for copy in v_copies:
        copy.wait()
    for at in range(count):
        c, h = at % blocks, at // blocks
        key = h // per_key
        span = slice(c * BLK, (c + 1) * BLK)
        t = inverse[at].astype(F32)
        erase = dot(
            (t * erase_row[at : at + 1, :]).astype(BF16), k_ref[span, key_lanes(key)]
        )
        write = dot((t * rate[at : at + 1, :]).astype(BF16), v_ref[span, head_lanes(h)])
        wu_ref[at, :, :DK] = erase.astype(BF16)
        wu_ref[at, :, DK:] = write.astype(BF16)
    for at in range(count):
        c, key = at % blocks, at // (per_key * blocks)
        tailed = (kt[key * blocks + c].astype(F32) * tail[at : at + 1, :]).astype(BF16)
        db[at] = dot(tailed, wu_ref[at]).astype(BF16)

    i = lax.broadcasted_iota(jnp.int32, (DK, DK), 0)
    j = lax.broadcasted_iota(jnp.int32, (DK, DK), 1)
    for h in range(heads):
        state[h, :, :DV] = jnp.zeros((DK, DV), F32)
        state[h, :, DV:] = jnp.where(i == j, 1.0, 0.0)
    for c in range(blocks):
        for h in range(heads):
            now = state[h]
            low = now.astype(BF16)
            at = h * blocks + c
            zc_ref[at] = low
            moved = dot(db[at, :, :DK], low)
            g = keep[at : at + 1, :]
            state[h, :, :DV] = g * now[:, :DV] - moved[:, :DV] + db[at, :, DK:].astype(F32)
            state[h, :, DV:] = g * now[:, DV:] - moved[:, DV:]
    for h in range(heads):
        end_ref[h] = state[h].astype(BF16)


def vmem(shape, dtype):
    return pltpu.VMEM(shape, dtype)


def in_hbm(array):
    return pltpu.with_memory_space_constraint(array, pltpu.HBM)


def in_vmem():
    return pl.BlockSpec(memory_space=pltpu.VMEM)


def shard_pass(part, parts, arrays, heads_here, per_key):
    tokens_here = arrays[3].shape[0]
    heads = heads_here // parts
    keys = heads // per_key
    blocks = tokens_here // BLK
    count = heads * blocks
    wide = DK + DV
    shapes = [
        vmem((count, BLK, wide), BF16),
        vmem((count, DK, wide), BF16),
        vmem((2 * count + blocks, BLK), F32),
        vmem((heads, DK, wide), BF16),
    ]
    scratch = [
        pltpu.VMEM((count, BLK), F32),
        pltpu.VMEM((count, BLK), F32),
        pltpu.VMEM((keys * blocks, BLK), F32),
        pltpu.VMEM((keys * blocks, DK, BLK), BF16),
        pltpu.VMEM((count, DK, wide), BF16),
        pltpu.VMEM((count, BLK), F32),
        pltpu.VMEM((heads, DK, wide), F32),
    ]
    if part == 0:
        shapes += [vmem(a.shape, a.dtype) for a in arrays]
        scratch += [pltpu.SemaphoreType.DMA((n,)) for n in (3, blocks, blocks)]
        arrays = [in_hbm(a) for a in arrays]
        space = pltpu.HBM
    else:
        space = pltpu.VMEM
    outs = pl.pallas_call(
        functools.partial(shard_kernel, part, parts, per_key, blocks, keys),
        in_specs=[pl.BlockSpec(memory_space=space)] * 5,
        out_specs=[in_vmem()] * len(shapes),
        out_shape=shapes,
        scratch_shapes=scratch,
        compiler_params=pltpu.CompilerParams(vmem_limit_bytes=24 * MIB),
        cost_estimate=pl.CostEstimate(
            flops=count * 18 * 2 * BLK**3, bytes_accessed=4 * MIB, transcendentals=0
        ),
        name="shard_pass",
    )(*arrays)
    return list(outs[:4]), outs[4:]


def local_kernel(
    part, parts, per_key, blocks, at_key, rows_ref, q_ref, k_ref, gate_ref, gain_ref, wu_ref, zc_ref,
    out_ref, carry_ref, gated_ref,
):
    count = per_key * blocks
    keys = wu_ref.shape[0] // count
    key = place_of(part, parts) * keys + at_key
    narrow = pl.ds(pl.multiple_of(key * DK, DK), DK)
    total = (rows_ref.shape[0] - blocks) // 2
    base = at_key * count
    cum = rows_ref[base : base + count, :]
    right = rows_ref[total + base : total + base + count, :]
    reset = rows_ref[2 * total :, :]
    cols = columns_of(jnp.concatenate([cum, reset], axis=0))
    units, inner, masks = [], [], []
    for c in range(blocks):
        span = slice(c * BLK, (c + 1) * BLK)
        query = q_ref[span, narrow].astype(F32)
        units.append(jnp.sum(query * query, axis=1, keepdims=True) + EPS)
        inner.append(dot_t(q_ref[span, narrow], k_ref[span, narrow]))
        masks.append(doc_mask(cols[:, count + c : count + c + 1], reset[c : c + 1, :], False))
    scores = []
    for at in range(count):
        c = at % blocks
        left = cols[:, at : at + 1] - 0.5 * jnp.log(units[c])
        gap = left - right[at : at + 1, :] + masks[c]
        scores.append((inner[c] * jnp.exp(gap)).astype(BF16))
    seen = [dot(scores[at], wu_ref[base + at]) for at in range(count)]
    for at in range(count):
        c, h = at % blocks, at // blocks
        span = slice(c * BLK, (c + 1) * BLK)
        wide = slice(h * DV, (h + 1) * DV)
        reset_col = cols[:, count + c : count + c + 1]
        keep = jnp.where(reset_col == 0.0, jnp.exp(cols[:, at : at + 1]), 0.0) * lax.rsqrt(units[c])
        g = (keep * q_ref[span, narrow].astype(F32) - seen[at][:, :DK]).astype(BF16)
        both = dot(g, zc_ref[base + at])
        out_ref[span, wide] = both[:, :DV] + seen[at][:, DK:]
        carry_ref[span, wide] = both[:, DV:].astype(BF16)
        first = pl.multiple_of((key * per_key + h) * DV, DV)
        gate = gate_ref[span, pl.ds(first, DV)].astype(F32)
        gated_ref[span, wide] = gain_ref[...] * (gate / (1.0 + jnp.exp(-gate)))


def local_pass(part, parts, at_key, rows, queries, key_rows, out_gate, gain, wu, zc, per_key):
    tokens_here = queries.shape[0]
    blocks = tokens_here // BLK
    count = per_key * blocks
    wide = per_key * DV
    return pl.pallas_call(
        functools.partial(local_kernel, part, parts, per_key, blocks, at_key),
        in_specs=[in_vmem()] * 7,
        out_specs=[in_vmem()] * 3,
        out_shape=[
            vmem((tokens_here, wide), F32),
            vmem((tokens_here, wide), BF16),
            vmem((tokens_here, wide), F32),
        ],
        compiler_params=pltpu.CompilerParams(vmem_limit_bytes=16 * MIB),
        cost_estimate=pl.CostEstimate(
            flops=count * 8 * 2 * BLK**3, bytes_accessed=4 * MIB, transcendentals=0
        ),
        name="local_pass",
    )(rows, queries, key_rows, out_gate, gain, wu, zc)


def finish_kernel(row, per_key, parts, order, *refs):
    me = lax.axis_index("head")
    keys_here = (len(refs) - parts - 3) // 3
    outs = refs[:keys_here]
    carries = refs[keys_here : 2 * keys_here]
    gates = refs[2 * keys_here : 3 * keys_here]
    starts = refs[3 * keys_here : 3 * keys_here + parts]
    weight_ref, send_ref, keep_ref = refs[3 * keys_here + parts :]
    rows = slice(row, row + send_ref.shape[0])
    heads = keys_here * per_key // parts
    normed = []
    for part in range(parts):
        pieces = []
        for head in range(heads):
            key, h = part * (keys_here // parts) + head // per_key, head % per_key
            span = slice(h * DV, (h + 1) * DV)
            seen = outs[key][rows, span] + dot(carries[key][rows, span], starts[part][head])
            spread = jnp.mean(seen * seen, axis=1, keepdims=True)
            pieces.append((seen * lax.rsqrt(spread + EPS) * gates[key][rows, span]).astype(BF16))
        normed.append(jnp.concatenate(pieces, axis=1))
    columns = weight_ref.shape[1] // len(order)
    sends = len(order) // 2
    for at, place in enumerate(order):
        first = pl.multiple_of((me ^ place) * columns, columns)
        total = None
        for part in range(parts):
            top = pl.multiple_of(place_of(part, parts) * (heads * DV), heads * DV)
            term = dot(normed[part], weight_ref[pl.ds(top, heads * DV), pl.ds(first, columns)])
            total = term if total is None else total + term
        to, slot = (send_ref, at - sends) if at >= sends else (keep_ref, at)
        to[:, slot * columns : (slot + 1) * columns] = total.astype(BF16)


def halving_order(size):
    def split(group, bit):
        if len(group) == 1:
            return group
        kept = [p for p in group if not p & bit]
        return split(kept, 2 * bit) + split([p for p in group if p & bit], 2 * bit)

    return split(list(range(size)), 1)


def finish_pass(row, rows, outs, carries, gates, starts, weight, per_key, devices):
    keys_here = len(outs)
    half = weight.shape[1] // 2
    return pl.pallas_call(
        functools.partial(
            finish_kernel, row, per_key, len(starts), halving_order(devices)
        ),
        in_specs=[in_vmem()] * (3 * keys_here + len(starts) + 1),
        out_specs=[in_vmem()] * 2,
        out_shape=[vmem((rows, half), BF16)] * 2,
        compiler_params=pltpu.CompilerParams(vmem_limit_bytes=16 * MIB),
        cost_estimate=pl.CostEstimate(
            flops=rows, bytes_accessed=rows, transcendentals=0
        ),
        name="finish_pass",
    )(*outs, *carries, *gates, *starts, weight)


def composed(later, earlier, h):
    return dot(later[h, :, DV:], earlier[h]) + later[h, :, :DV].astype(F32)


def pair_kernel(mine_ref, got_ref, both_ref, begun_ref):
    odd = lax.rem(lax.axis_index("seq"), 2) == 1

    def join(second, first):
        for h in range(both_ref.shape[0]):
            moved = dot(second[h, :, DV:], first[h])
            begun = (moved[:, :DV] + second[h, :, :DV].astype(F32)).astype(BF16)
            begun_ref[h] = begun
            both_ref[h, :, :DV] = begun
            both_ref[h, :, DV:] = moved[:, DV:].astype(BF16)

    @pl.when(odd)
    def _():
        join(mine_ref, got_ref)

    @pl.when(jnp.logical_not(odd))
    def _():
        join(got_ref, mine_ref)


def step_kernel(later_ref, earlier_ref, out_ref):
    for h in range(out_ref.shape[0]):
        out_ref[h] = composed(later_ref, earlier_ref, h).astype(BF16)


def last_kernel(
    mine_ref, got_ref, first_ref, before_ref, near_ref, far_ref, own_ref, other_ref
):
    odd = lax.rem(lax.axis_index("seq"), 2) == 1
    pair = lax.div(lax.axis_index("seq"), 2)

    def fill(first, here_ref, then_ref):
        for h in range(own_ref.shape[0]):
            here = composed(before_ref, far_ref, h).astype(BF16)
            here = jnp.where(pair == 2, near_ref[h], here)
            here_ref[h] = jnp.where(pair == 1, first_ref[h], here)
        for h in range(own_ref.shape[0]):
            then_ref[h] = composed(first, here_ref, h).astype(BF16)

    @pl.when(odd)
    def _():
        fill(got_ref, other_ref, own_ref)

    @pl.when(jnp.logical_not(odd))
    def _():
        fill(mine_ref, own_ref, other_ref)


def small_call(kernel, name, outs, *arrays):
    heads = arrays[0].shape[0]
    return pl.pallas_call(
        kernel,
        in_specs=[in_vmem()] * len(arrays),
        out_specs=[in_vmem()] * len(outs),
        out_shape=[vmem(a.shape, a.dtype) for a in outs],
        compiler_params=pltpu.CompilerParams(vmem_limit_bytes=4 * MIB),
        cost_estimate=pl.CostEstimate(
            flops=heads * 4 * DK**3, bytes_accessed=MIB, transcendentals=0
        ),
        name=name,
    )(*arrays)


def step_call(later, earlier):
    return small_call(
        step_kernel, "step", [jax.ShapeDtypeStruct(earlier.shape, BF16)], later, earlier
    )[0]


def route(axis, target):
    size = lax.axis_size(axis)
    return [(i, target(i)) for i in range(size) if target(i) is not None]


def exchanged(mine, got, work):
    state = jax.ShapeDtypeStruct(mine.shape[:2] + (DV,), BF16)
    both, begun = small_call(
        pair_kernel, "pair", [jax.ShapeDtypeStruct(mine.shape, BF16), state], mine, got
    )
    first = lax.ppermute(begun, "seq", [(0, 2), (1, 3)])
    before = lax.ppermute(both, "seq", [(4, 6), (5, 7)])
    first = work(work(first))
    third = step_call(both, first)
    near = lax.ppermute(third, "seq", [(2, 4), (3, 5)])
    far = work(lax.ppermute(third, "seq", [(2, 6), (3, 7)]))
    own, other = small_call(
        last_kernel, "last", [state] * 2, mine, got, first, before, near, far
    )
    return own, work(lax.ppermute(other, "seq", route("seq", lambda i: i ^ 1)))


def handed_on(end):
    size = lax.axis_size("seq")
    onward = route("seq", lambda i: i + 1 if i + 1 < size else None)

    def hop(step, state):
        return lax.ppermute(step_call(end, state), "seq", onward)

    return lax.fori_loop(0, size - 1, hop, jnp.zeros(end.shape[:2] + (DV,), BF16))


def assemble_kernel(pieces, *refs):
    kept, got, out_ref = refs[:pieces], refs[pieces : 2 * pieces], refs[2 * pieces]
    row = 0
    for keep_ref, got_ref in zip(kept, got):
        rows, columns = got_ref.shape
        total = keep_ref[:, :columns].astype(F32) + got_ref[...].astype(F32)
        out_ref[row : row + rows, :] = total.astype(BF16)
        row += rows


def assemble(kept, got):
    shape = (sum(piece.shape[0] for piece in got), got[0].shape[1])
    return pl.pallas_call(
        functools.partial(assemble_kernel, len(got)),
        grid=(1,),
        in_specs=[in_vmem()] * (2 * len(got)),
        out_specs=pl.BlockSpec(shape, lambda i: (0, 0)),
        out_shape=jax.ShapeDtypeStruct(shape, BF16),
        compiler_params=pltpu.CompilerParams(vmem_limit_bytes=8 * MIB),
        name="assemble",
    )(*kept, *got)


def local(
    queries, key_rows, value_rows, out_gate, write_rate, log_gate, doc_start, norm_gain, out_weight
):
    tokens_here = queries.shape[0]
    heads_here = value_rows.shape[1] // DV
    keys_here = key_rows.shape[1] // DK
    per_key = heads_here // keys_here
    devices = lax.axis_size("head")
    parts = 2 if lax.axis_size("seq") == 8 and keys_here % 2 == 0 else 1
    keys = keys_here // parts
    starts = doc_start.reshape(tokens_here // BLK, BLK)
    gain = norm_gain.reshape(1, DV)
    queries, out_gate, weight, gain = (
        pltpu.with_memory_space_constraint(a, pltpu.VMEM)
        for a in (queries, out_gate, out_weight, gain)
    )
    shards, got = [], None
    held = [log_gate, write_rate, starts, key_rows, value_rows]
    for part in range(parts):
        shard, here = shard_pass(part, parts, held, heads_here, per_key)
        shards.append(shard)
        if part == 0:
            held = here
            nearby_keys = held[3]
            if parts == 2:
                got = lax.ppermute(shard[3], "seq", route("seq", lambda i: i ^ 1))
    outs, carries, gates = [], [], []

    def work(coming):
        at = len(outs)
        if at == keys_here:
            return coming
        wu, zc, rows, _ = shards[at // keys]
        out, carry, gate = local_pass(
            at // keys, parts, at % keys, rows, queries, nearby_keys, out_gate, gain, wu, zc, per_key
        )
        coming, out, carry, gate = lax.optimization_barrier((coming, out, carry, gate))
        outs.append(out)
        carries.append(carry)
        gates.append(gate)
        return coming

    if parts == 2:
        mine = shards[1][3]
        rows, mine = lax.optimization_barrier((shards[0][2], mine))
        shards[0][2] = rows
        own, back = exchanged(mine, got, work)
        states = [back, own]
    else:
        states = [handed_on(shards[0][3])]
    while len(outs) < keys_here:
        states[0] = work(states[0])

    unit = tokens_here // 16
    sizes = [unit * share for share in (4, 4, 4, 4)]
    firsts = [sum(sizes[:index]) for index in range(len(sizes))]
    kept, arrived = [], []
    for first, rows in zip(firsts, sizes):
        send, keep = finish_pass(
            first, rows, outs, carries, gates, states, weight, per_key, devices
        )
        bit = 1
        while bit < devices:
            got = lax.ppermute(send, "head", route("head", lambda i: i ^ bit))
            bit *= 2
            if bit < devices:
                keep = keep.astype(F32) + got.astype(F32)
                width = keep.shape[1] // 2
                send = keep[:, width:].astype(BF16)
                keep = keep[:, :width] if 2 * bit < devices else keep
        kept.append(keep)
        arrived.append(got)
    return assemble(kept, arrived)


def solution(mesh):
    placed = (
        P("seq", "head"),
        P("seq", "head"),
        P("seq", "head"),
        P("seq", "head"),
        P("head", "seq"),
        P("head", "seq"),
        P("seq"),
        P(),
        P("head", None),
    )
    return jax.shard_map(
        local, mesh=mesh, in_specs=placed, out_specs=P("seq", "head"), check_vma=False
    )
```

```python
import functools

import jax
import jax.numpy as jnp
from jax import lax
from jax.experimental import pallas as pl
from jax.experimental.pallas import tpu as pltpu
from jax.sharding import PartitionSpec as P

DK = 128
DV = 128
BLK = 128
SUB = 16
EPS = 1e-06
FAR = -1e30
F32 = jnp.float32
BF16 = jnp.bfloat16
MIB = 1024 * 1024


def dot(a, b):
    return jnp.dot(a, b, preferred_element_type=F32)


def dot_t(a, b):
    return lax.dot_general(a, b, (((1,), (1,)), ((), ())), preferred_element_type=F32)


def running_sum(values):
    lane = lax.broadcasted_iota(jnp.int32, values.shape, 1)
    step = 1
    while step < BLK:
        values = values + jnp.where(lane >= step, pltpu.roll(values, step, 1), 0.0)
        step *= 2
    return values


def columns_of(rows):
    pad = BLK - rows.shape[0]
    return jnp.transpose(jnp.concatenate([rows, jnp.zeros((pad, BLK), F32)], axis=0))


def doc_mask(reset_col, reset_row, strict):
    i = lax.broadcasted_iota(jnp.int32, (BLK, BLK), 0)
    j = lax.broadcasted_iota(jnp.int32, (BLK, BLK), 1)
    below = (i > j) if strict else (i >= j)
    return jnp.where(below & (reset_col == reset_row), 0.0, FAR)


def place_of(part, parts):
    if parts == 1:
        return 0
    odd = lax.rem(lax.axis_index("seq"), 2)
    return odd if part == 1 else 1 - odd


def small_inverses(lower, count):
    lane = lax.broadcasted_iota(jnp.int32, (SUB, BLK), 1)
    packed = []
    for m in lower:
        kept = m[:SUB]
        for b in range(1, BLK // SUB):
            kept = jnp.where(lane // SUB == b, m[b * SUB : (b + 1) * SUB], kept)
        packed.append(kept.astype(BF16))
    packed = jnp.concatenate(packed, axis=0)
    i = lax.broadcasted_iota(jnp.int32, (BLK, BLK), 0)
    j = lax.broadcasted_iota(jnp.int32, (BLK, BLK), 1)
    same = i // SUB == j // SUB
    place = lax.broadcasted_iota(jnp.int32, (count, SUB, BLK), 1)
    lanes = lax.broadcasted_iota(jnp.int32, (count, SUB, BLK), 2)
    found = jnp.where(place == lanes % SUB, 1.0, 0.0)
    for m in range(0, SUB, 2):
        spread = [jnp.where(same & (i % SUB == m + d), 1.0, 0.0).astype(BF16) for d in range(2)]
        pair = dot(packed, jnp.concatenate(spread, axis=1)).reshape(count, SUB, 2 * BLK)
        for d in range(2):
            if m + d < SUB - 1:
                found = found - pair[:, :, d * BLK : (d + 1) * BLK] * found[:, m + d : m + d + 1, :]
    return found.astype(BF16)


def odd_rows(matrix, size):
    return jnp.concatenate(
        [matrix[p : p + size] for p in range(size, BLK, 2 * size)], axis=0
    )


def with_odd_rows(matrix, rows, size):
    parts = []
    for p in range(0, BLK, 2 * size):
        parts.append(matrix[p : p + size])
        parts.append(rows[p // 2 : p // 2 + size])
    return jnp.concatenate(parts, axis=0)


def shard_kernel(
    part, parts, per_key, blocks, keys, devices, *refs
):
    if part == 0:
        log_in, rate_in, start_in, k_in, v_in, w_in = refs[:6]
        wu_ref, zc_ref, rows_ref, end_ref, log_ref, rate_ref, start_ref, k_ref, v_ref = refs[6:15]
        w_keep, w_give = refs[15:17]
    else:
        log_ref, rate_ref, start_ref, k_ref, v_ref, wu_ref, zc_ref, rows_ref, end_ref = refs[:9]
    logs, rates, norms, kt, db, keep, state = refs[len(refs) - 7 :] if part else refs[17:24]
    mine = place_of(part, parts)
    small_copies, k_copies, v_copies = [], [], []
    if part == 0:
        small_sems, k_sems, other_sems, v_sems, w_sems = refs[24:]
        for at, (ref, here) in enumerate(
            ((log_in, log_ref), (rate_in, rate_ref), (start_in, start_ref))
        ):
            small_copies.append(pltpu.make_async_copy(ref, here, small_sems.at[at]))
        width = keys * DK
        for place, copies, sems in ((mine, k_copies, k_sems), (1 - mine, v_copies, other_sems)):
            if parts == 1 and copies is v_copies:
                continue
            lanes = pl.ds(pl.multiple_of(place * width, width), width)
            for c in range(blocks):
                at = (slice(c * BLK, (c + 1) * BLK), lanes)
                copies.append(pltpu.make_async_copy(k_in.at[at], k_ref.at[at], sems.at[c]))
        for c in range(blocks):
            span = slice(c * BLK, (c + 1) * BLK)
            v_copies.append(pltpu.make_async_copy(v_in.at[span], v_ref.at[span], v_sems.at[c]))
        w_copies = []
        order = halving_order(devices)
        columns = w_in.shape[1] // devices
        for at, place in enumerate(order):
            first = pl.multiple_of((lax.axis_index("head") ^ place) * columns, columns)
            to, slot = (w_keep, at) if at < devices // 2 else (w_give, at - devices // 2)
            w_copies.append(
                pltpu.make_async_copy(
                    w_in.at[:, pl.ds(first, columns)],
                    to.at[:, slot * columns : (slot + 1) * columns],
                    w_sems.at[at],
                )
            )
        for copy in small_copies + k_copies:
            copy.start()
        for copy in small_copies:
            copy.wait()
    key_lanes = lambda key: pl.ds(pl.multiple_of((mine * keys + key) * DK, DK), DK)
    head_lanes = lambda h: pl.ds(pl.multiple_of((mine * keys * per_key + h) * DV, DV), DV)
    heads = keys * per_key
    count = heads * blocks
    for place in range(parts):

        @pl.when(mine == place)
        def _():
            for h in range(heads):
                head = place * heads + h
                for c in range(blocks):
                    at = h * blocks + c
                    span = slice(c * BLK, (c + 1) * BLK)
                    logs[at : at + 1, :] = log_ref[head : head + 1, span]
                    rates[at : at + 1, :] = rate_ref[head : head + 1, span]

    starts = start_ref[...].astype(F32)
    sums = running_sum(jnp.concatenate([logs[...], starts], axis=0))
    cum, reset = sums[:count], sums[count:]
    inner = []
    for copy in k_copies:
        copy.wait()
    for copy in v_copies:
        copy.start()
    if part == 0:
        for copy in w_copies:
            copy.start()
    for key in range(keys):
        for c in range(blocks):
            rows = k_ref[c * BLK : (c + 1) * BLK, key_lanes(key)]
            flipped = jnp.transpose(rows.astype(F32))
            turned = flipped.astype(BF16)
            kt[key * blocks + c] = turned
            norms[key * blocks + c : key * blocks + c + 1, :] = jnp.sum(
                flipped * flipped, axis=0, keepdims=True
            )
            inner.append(dot(rows, turned))
    reset_cols = columns_of(reset)
    masks = [doc_mask(reset_cols[:, c : c + 1], reset[c : c + 1, :], True) for c in range(blocks)]

    squares = norms[...] + EPS
    squares = jnp.concatenate(
        [squares[(h // per_key) * blocks : (h // per_key + 1) * blocks] for h in range(heads)], axis=0
    )
    scale = lax.rsqrt(squares)
    log_scale = -0.5 * jnp.log(squares)
    resets = jnp.concatenate([reset] * heads, axis=0)
    rate = rates[...]
    last = cum[:, BLK - 1 :]
    last_reset = resets[:, BLK - 1 :]
    left_cols = columns_of(cum + jnp.log(rate) + log_scale)
    right = cum - log_scale
    head_keep = jnp.where(resets == 0.0, jnp.exp(cum), 0.0)
    tail = jnp.where(resets == last_reset, jnp.exp(last - cum), 0.0) * scale
    erase_row = rate * head_keep * scale
    keep[...] = jnp.broadcast_to(jnp.where(last_reset == 0.0, jnp.exp(last), 0.0), (count, BLK))
    rows_ref[0:count, :] = cum
    rows_ref[count : 2 * count, :] = right
    rows_ref[2 * count :, :] = reset

    lower = []
    for at in range(count):
        c = at % blocks
        gap = left_cols[:, at : at + 1] - right[at : at + 1, :] + masks[c]
        lower.append(inner[at // (per_key * blocks) * blocks + c] * jnp.exp(gap))
    packed = small_inverses(lower, count)
    lower = [m.astype(BF16) for m in lower]
    lane = lax.broadcasted_iota(jnp.int32, (SUB, BLK), 1)
    zero = jnp.zeros((SUB, BLK), BF16)
    ones = [jnp.where(lane // SUB == b, 1.0, 0.0).astype(BF16) for b in range(BLK // SUB)]
    inverse = [
        jnp.concatenate([packed[at] * ones[b] for b in range(BLK // SUB)], axis=0)
        for at in range(count)
    ]
    size = SUB
    while size < BLK:
        i = lax.broadcasted_iota(jnp.int32, (BLK // 2, BLK), 0)
        j = lax.broadcasted_iota(jnp.int32, (BLK // 2, BLK), 1)
        reach = jnp.where(j // size == 2 * (i // size), 1.0, 0.0).astype(BF16)
        odd = [odd_rows(t, size) for t in inverse]
        half = [dot(o, m).astype(BF16) * reach for o, m in zip(odd, lower)]
        fresh = [o - dot(f, t).astype(BF16) for o, f, t in zip(odd, half, inverse)]
        inverse = [with_odd_rows(t, f, size) for t, f in zip(inverse, fresh)]
        size *= 2
    for copy in v_copies:
        copy.wait()
    for at in range(count):
        c, h = at % blocks, at // blocks
        key = h // per_key
        span = slice(c * BLK, (c + 1) * BLK)
        t = inverse[at].astype(F32)
        erase = dot(
            (t * erase_row[at : at + 1, :]).astype(BF16), k_ref[span, key_lanes(key)]
        )
        write = dot((t * rate[at : at + 1, :]).astype(BF16), v_ref[span, head_lanes(h)])
        wu_ref[at, :, :DK] = erase.astype(BF16)
        wu_ref[at, :, DK:] = write.astype(BF16)
    for at in range(count):
        c, key = at % blocks, at // (per_key * blocks)
        tailed = (kt[key * blocks + c].astype(F32) * tail[at : at + 1, :]).astype(BF16)
        db[at] = dot(tailed, wu_ref[at]).astype(BF16)

    i = lax.broadcasted_iota(jnp.int32, (DK, DK), 0)
    j = lax.broadcasted_iota(jnp.int32, (DK, DK), 1)
    for h in range(heads):
        state[h, :, :DV] = jnp.zeros((DK, DV), F32)
        state[h, :, DV:] = jnp.where(i == j, 1.0, 0.0)
    for c in range(blocks):
        for h in range(heads):
            now = state[h]
            low = now.astype(BF16)
            at = h * blocks + c
            zc_ref[at] = low
            moved = dot(db[at, :, :DK], low)
            g = keep[at : at + 1, :]
            state[h, :, :DV] = g * now[:, :DV] - moved[:, :DV] + db[at, :, DK:].astype(F32)
            state[h, :, DV:] = g * now[:, DV:] - moved[:, DV:]
    for h in range(heads):
        end_ref[h] = state[h].astype(BF16)
    if part == 0:
        for copy in w_copies:
            copy.wait()


def vmem(shape, dtype):
    return pltpu.VMEM(shape, dtype)


def in_hbm(array):
    return pltpu.with_memory_space_constraint(array, pltpu.HBM)


def in_vmem():
    return pl.BlockSpec(memory_space=pltpu.VMEM)


def shard_pass(part, parts, arrays, heads_here, per_key, devices):
    tokens_here = arrays[3].shape[0]
    heads = heads_here // parts
    keys = heads // per_key
    blocks = tokens_here // BLK
    count = heads * blocks
    wide = DK + DV
    shapes = [
        vmem((count, BLK, wide), BF16),
        vmem((count, DK, wide), BF16),
        vmem((2 * count + blocks, BLK), F32),
        vmem((heads, DK, wide), BF16),
    ]
    scratch = [
        pltpu.VMEM((count, BLK), F32),
        pltpu.VMEM((count, BLK), F32),
        pltpu.VMEM((keys * blocks, BLK), F32),
        pltpu.VMEM((keys * blocks, DK, BLK), BF16),
        pltpu.VMEM((count, DK, wide), BF16),
        pltpu.VMEM((count, BLK), F32),
        pltpu.VMEM((heads, DK, wide), F32),
    ]
    if part == 0:
        depth, wide = arrays[5].shape
        shapes += [vmem(a.shape, a.dtype) for a in arrays[:5]] + [vmem((depth, wide // 2), BF16)] * 2
        scratch += [pltpu.SemaphoreType.DMA((n,)) for n in (3, blocks, blocks, blocks, devices)]
        arrays = [in_hbm(a) for a in arrays]
        space = pltpu.HBM
    else:
        space = pltpu.VMEM
    outs = pl.pallas_call(
        functools.partial(shard_kernel, part, parts, per_key, blocks, keys, devices),
        in_specs=[pl.BlockSpec(memory_space=space)] * len(arrays),
        out_specs=[in_vmem()] * len(shapes),
        out_shape=shapes,
        scratch_shapes=scratch,
        compiler_params=pltpu.CompilerParams(vmem_limit_bytes=24 * MIB),
        cost_estimate=pl.CostEstimate(
            flops=count * 18 * 2 * BLK**3, bytes_accessed=4 * MIB, transcendentals=0
        ),
        name="shard_pass",
    )(*arrays)
    return list(outs[:4]), outs[4:]


def local_kernel(
    part, parts, per_key, blocks, at_key, rows_ref, q_ref, k_ref, gate_ref, gain_ref, wu_ref, zc_ref,
    out_ref, carry_ref, gated_ref,
):
    count = per_key * blocks
    keys = wu_ref.shape[0] // count
    key = place_of(part, parts) * keys + at_key
    narrow = pl.ds(pl.multiple_of(key * DK, DK), DK)
    total = (rows_ref.shape[0] - blocks) // 2
    base = at_key * count
    cum = rows_ref[base : base + count, :]
    right = rows_ref[total + base : total + base + count, :]
    reset = rows_ref[2 * total :, :]
    cols = columns_of(jnp.concatenate([cum, reset], axis=0))
    units, inner, masks = [], [], []
    for c in range(blocks):
        span = slice(c * BLK, (c + 1) * BLK)
        query = q_ref[span, narrow].astype(F32)
        units.append(jnp.sum(query * query, axis=1, keepdims=True) + EPS)
        inner.append(dot_t(q_ref[span, narrow], k_ref[span, narrow]))
        masks.append(doc_mask(cols[:, count + c : count + c + 1], reset[c : c + 1, :], False))
    scores = []
    for at in range(count):
        c = at % blocks
        left = cols[:, at : at + 1] - 0.5 * jnp.log(units[c])
        gap = left - right[at : at + 1, :] + masks[c]
        scores.append((inner[c] * jnp.exp(gap)).astype(BF16))
    seen = [dot(scores[at], wu_ref[base + at]) for at in range(count)]
    for at in range(count):
        c, h = at % blocks, at // blocks
        span = slice(c * BLK, (c + 1) * BLK)
        wide = slice(h * DV, (h + 1) * DV)
        reset_col = cols[:, count + c : count + c + 1]
        keep = jnp.where(reset_col == 0.0, jnp.exp(cols[:, at : at + 1]), 0.0) * lax.rsqrt(units[c])
        g = (keep * q_ref[span, narrow].astype(F32) - seen[at][:, :DK]).astype(BF16)
        both = dot(g, zc_ref[base + at])
        out_ref[span, wide] = both[:, :DV] + seen[at][:, DK:]
        carry_ref[span, wide] = both[:, DV:].astype(BF16)
        first = pl.multiple_of((key * per_key + h) * DV, DV)
        gate = gate_ref[span, pl.ds(first, DV)].astype(F32)
        gated_ref[span, wide] = gain_ref[...] * (gate / (1.0 + jnp.exp(-gate)))


def local_pass(part, parts, at_key, rows, queries, key_rows, out_gate, gain, wu, zc, per_key):
    tokens_here = queries.shape[0]
    blocks = tokens_here // BLK
    count = per_key * blocks
    wide = per_key * DV
    return pl.pallas_call(
        functools.partial(local_kernel, part, parts, per_key, blocks, at_key),
        in_specs=[in_vmem()] * 7,
        out_specs=[in_vmem()] * 3,
        out_shape=[
            vmem((tokens_here, wide), F32),
            vmem((tokens_here, wide), BF16),
            vmem((tokens_here, wide), F32),
        ],
        compiler_params=pltpu.CompilerParams(vmem_limit_bytes=16 * MIB),
        cost_estimate=pl.CostEstimate(
            flops=count * 8 * 2 * BLK**3, bytes_accessed=4 * MIB, transcendentals=0
        ),
        name="local_pass",
    )(rows, queries, key_rows, out_gate, gain, wu, zc)


def norm_kernel(row, per_key, parts, *refs):
    keys_here = (len(refs) - parts - 1) // 3
    outs = refs[:keys_here]
    carries = refs[keys_here : 2 * keys_here]
    gates = refs[2 * keys_here : 3 * keys_here]
    starts, normed_ref = refs[3 * keys_here : -1], refs[-1]
    rows = slice(row, row + normed_ref.shape[0])
    heads = keys_here * per_key // parts
    for key in range(keys_here):
        for h in range(per_key):
            head = key * per_key + h
            span = slice(h * DV, (h + 1) * DV)
            start = starts[head // heads][head % heads]
            seen = outs[key][rows, span] + dot(carries[key][rows, span], start)
            spread = jnp.mean(seen * seen, axis=1, keepdims=True)
            normed = seen * lax.rsqrt(spread + EPS) * gates[key][rows, span]
            normed_ref[:, head * DV : (head + 1) * DV] = normed.astype(BF16)


def norm_pass(row, rows, outs, carries, gates, starts, per_key):
    arrays = (*outs, *carries, *gates, *starts)
    return pl.pallas_call(
        functools.partial(norm_kernel, row, per_key, len(starts)),
        in_specs=[in_vmem()] * len(arrays),
        out_specs=in_vmem(),
        out_shape=vmem((rows, len(outs) * per_key * DV), BF16),
        compiler_params=pltpu.CompilerParams(vmem_limit_bytes=8 * MIB),
        cost_estimate=pl.CostEstimate(flops=rows, bytes_accessed=rows, transcendentals=0),
        name="norm_pass",
    )(*arrays)


def project_kernel(parts, own_ref, got_ref, kept_ref, given_ref, keep_ref, send_ref):
    heads_wide = own_ref.shape[1] // parts
    width = keep_ref.shape[1]
    for to, columns in ((send_ref, slice(width, 2 * width)), (keep_ref, slice(0, width))):
        total = None
        for normed, weight in ((own_ref, kept_ref), (got_ref, given_ref)):
            for part in range(parts):
                top = pl.multiple_of(place_of(part, parts) * heads_wide, heads_wide)
                term = dot(
                    normed[:, part * heads_wide : (part + 1) * heads_wide],
                    weight[pl.ds(top, heads_wide), columns],
                )
                total = term if total is None else total + term
        to[...] = total.astype(to.dtype)


def project(normed, got, weight_kept, weight_got, parts):
    rows, width = normed.shape[0], weight_kept.shape[1] // 2
    return pl.pallas_call(
        functools.partial(project_kernel, parts),
        in_specs=[in_vmem()] * 4,
        out_specs=[in_vmem()] * 2,
        out_shape=[vmem((rows, width), F32), vmem((rows, width), BF16)],
        compiler_params=pltpu.CompilerParams(vmem_limit_bytes=8 * MIB),
        cost_estimate=pl.CostEstimate(flops=rows, bytes_accessed=rows, transcendentals=0),
        name="project",
    )(normed, got, weight_kept, weight_got)


def halving_order(size):
    def split(group, bit):
        if len(group) == 1:
            return group
        kept = [p for p in group if not p & bit]
        return split(kept, 2 * bit) + split([p for p in group if p & bit], 2 * bit)

    return split(list(range(size)), 1)


def composed(state, move, earlier):
    return (dot(move, earlier) + state.astype(F32)).astype(BF16)


def pair_kernel(mine_ref, got_ref, begun_ref, move_ref):
    odd = lax.rem(lax.axis_index("seq"), 2) == 1

    def join(second, first):
        for h in range(begun_ref.shape[0]):
            moved = dot(second[h, :, DV:], first[h])
            begun_ref[h] = (moved[:, :DV] + second[h, :, :DV].astype(F32)).astype(BF16)
            move_ref[h] = moved[:, DV:].astype(BF16)

    @pl.when(odd)
    def _():
        join(mine_ref, got_ref)

    @pl.when(jnp.logical_not(odd))
    def _():
        join(got_ref, mine_ref)


def step_kernel(state_ref, move_ref, earlier_ref, out_ref):
    for h in range(out_ref.shape[0]):
        out_ref[h] = composed(state_ref[h], move_ref[h], earlier_ref[h])


def last_kernel(mine_ref, got_ref, before_ref, turn_ref, near_ref, far_ref, own_ref, other_ref):
    odd = lax.rem(lax.axis_index("seq"), 2) == 1
    pair = lax.div(lax.axis_index("seq"), 2)

    def fill(first, here_ref, then_ref):
        for h in range(own_ref.shape[0]):
            before = before_ref[h]
            here = composed(before, turn_ref[h], far_ref[h])
            here = jnp.where(pair == 2, near_ref[h], here)
            here = jnp.where(pair == 1, before, here)
            here_ref[h] = jnp.where(pair == 0, jnp.zeros_like(here), here)
        for h in range(own_ref.shape[0]):
            then_ref[h] = composed(first[h, :, :DV], first[h, :, DV:], here_ref[h])

    @pl.when(odd)
    def _():
        fill(got_ref, other_ref, own_ref)

    @pl.when(jnp.logical_not(odd))
    def _():
        fill(mine_ref, own_ref, other_ref)


def small_call(kernel, name, outs, *arrays):
    heads = arrays[0].shape[0]
    return pl.pallas_call(
        kernel,
        in_specs=[in_vmem()] * len(arrays),
        out_specs=[in_vmem()] * len(outs),
        out_shape=[vmem(a.shape, a.dtype) for a in outs],
        compiler_params=pltpu.CompilerParams(vmem_limit_bytes=4 * MIB),
        cost_estimate=pl.CostEstimate(
            flops=heads * 4 * DK**3, bytes_accessed=MIB, transcendentals=0
        ),
        name=name,
    )(*arrays)


def step_call(state, move, earlier):
    shape = jax.ShapeDtypeStruct(earlier.shape, BF16)
    return small_call(step_kernel, "step", [shape], state, move, earlier)[0]


def route(axis, target):
    size = lax.axis_size(axis)
    return [(i, target(i)) for i in range(size) if target(i) is not None]


def exchanged(mine, got, work):
    state = jax.ShapeDtypeStruct(mine.shape[:2] + (DV,), BF16)
    begun, move = small_call(pair_kernel, "pair", [state] * 2, mine, got)
    before = lax.ppermute(begun, "seq", route("seq", lambda i: i ^ 2))
    turn = lax.ppermute(move, "seq", route("seq", lambda i: i ^ 2))
    before = work(before)
    third = step_call(begun, move, before)
    near = lax.ppermute(third, "seq", route("seq", lambda i: i ^ 6 if i // 2 in (1, 2) else i ^ 1))
    far = lax.ppermute(third, "seq", route("seq", lambda i: i ^ 4 if i // 2 in (1, 3) else i ^ 1))
    turn, far = work((turn, far)), work(far)
    own, other = small_call(
        last_kernel, "last", [state] * 2, mine, got, before, turn, near, far
    )
    return own, work(lax.ppermute(other, "seq", route("seq", lambda i: i ^ 1)))


def handed_on(end):
    size = lax.axis_size("seq")
    onward = route("seq", lambda i: i + 1 if i + 1 < size else None)

    def hop(step, state):
        return lax.ppermute(step_call(end[:, :, :DV], end[:, :, DV:], state), "seq", onward)

    return lax.fori_loop(0, size - 1, hop, jnp.zeros(end.shape[:2] + (DV,), BF16))


def assemble_kernel(pieces, *refs):
    kept, got, out_ref = refs[:pieces], refs[pieces : 2 * pieces], refs[2 * pieces]
    row = 0
    for keep_ref, got_ref in zip(kept, got):
        rows, columns = got_ref.shape
        total = keep_ref[:, :columns].astype(F32) + got_ref[...].astype(F32)
        out_ref[row : row + rows, :] = total.astype(BF16)
        row += rows


def assemble(kept, got):
    shape = (sum(piece.shape[0] for piece in got), got[0].shape[1])
    return pl.pallas_call(
        functools.partial(assemble_kernel, len(got)),
        grid=(1,),
        in_specs=[in_vmem()] * (2 * len(got)),
        out_specs=pl.BlockSpec(shape, lambda i: (0, 0)),
        out_shape=jax.ShapeDtypeStruct(shape, BF16),
        compiler_params=pltpu.CompilerParams(vmem_limit_bytes=8 * MIB),
        name="assemble",
    )(*kept, *got)


def local(
    queries, key_rows, value_rows, out_gate, write_rate, log_gate, doc_start, norm_gain, out_weight
):
    tokens_here = queries.shape[0]
    heads_here = value_rows.shape[1] // DV
    keys_here = key_rows.shape[1] // DK
    per_key = heads_here // keys_here
    devices = lax.axis_size("head")
    parts = 2 if lax.axis_size("seq") == 8 and keys_here % 2 == 0 else 1
    keys = keys_here // parts
    starts = doc_start.reshape(tokens_here // BLK, BLK)
    gain = norm_gain.reshape(1, DV)
    queries, out_gate, gain = (
        pltpu.with_memory_space_constraint(a, pltpu.VMEM) for a in (queries, out_gate, gain)
    )
    shards, got = [], None
    held = [log_gate, write_rate, starts, key_rows, value_rows, out_weight]
    for part in range(parts):
        shard, here = shard_pass(part, parts, held, heads_here, per_key, devices)
        shards.append(shard)
        if part == 0:
            held, (weight_kept, weight_given) = here[:5], here[5:]
            nearby_keys = held[3]
            weight_got = lax.ppermute(weight_given, "head", route("head", lambda i: i ^ 1))
            if parts == 2:
                got = lax.ppermute(shard[3], "seq", route("seq", lambda i: i ^ 1))
    outs, carries, gates = [], [], []

    def work(coming):
        at = len(outs)
        if at == keys_here:
            return coming
        wu, zc, rows, _ = shards[at // keys]
        if isinstance(coming, tuple):
            rows, coming = lax.optimization_barrier((rows, coming[0]))
        out, carry, gate = local_pass(
            at // keys, parts, at % keys, rows, queries, nearby_keys, out_gate, gain, wu, zc, per_key
        )
        coming, out, carry, gate = lax.optimization_barrier((coming, out, carry, gate))
        outs.append(out)
        carries.append(carry)
        gates.append(gate)
        return coming

    if parts == 2:
        mine = shards[1][3]
        rows, mine = lax.optimization_barrier((shards[0][2], mine))
        shards[0][2] = rows
        own, back = exchanged(mine, got, work)
        states = [back, own]
    else:
        states = [handed_on(shards[0][3])]
    while len(outs) < keys_here:
        states[0] = work(states[0])

    unit = tokens_here // 16
    sizes = [unit * share for share in (4, 4, 4, 4)]
    firsts = [sum(sizes[:index]) for index in range(len(sizes))]
    normed = [
        norm_pass(first, rows, outs, carries, gates, states, per_key)
        for first, rows in zip(firsts, sizes)
    ]
    kept, arrived = [], []
    for piece in normed:
        across = lax.ppermute(piece, "head", route("head", lambda i: i ^ 1))
        keep, send = project(piece, across, weight_kept, weight_got, parts)
        bit = 2
        while bit < devices:
            got = lax.ppermute(send, "head", route("head", lambda i: i ^ bit))
            bit *= 2
            if bit < devices:
                keep = keep + got.astype(F32)
                width = keep.shape[1] // 2
                send = keep[:, width:].astype(BF16)
                keep = keep[:, :width]
        kept.append(keep)
        arrived.append(got)
    return assemble(kept, arrived)


def solution(mesh):
    placed = (
        P("seq", "head"),
        P("seq", "head"),
        P("seq", "head"),
        P("seq", "head"),
        P("head", "seq"),
        P("head", "seq"),
        P("seq"),
        P(),
        P("head", None),
    )
    return jax.shard_map(
        local, mesh=mesh, in_specs=placed, out_specs=P("seq", "head"), check_vma=False
    )
```

```python
import functools

import jax
import jax.numpy as jnp
from jax import lax
from jax.experimental import pallas as pl
from jax.experimental.pallas import tpu as pltpu
from jax.sharding import PartitionSpec as P

DK = 128
DV = 128
BLK = 128
SUB = 16
EPS = 1e-06
FAR = -1e30
F32 = jnp.float32
BF16 = jnp.bfloat16
MIB = 1024 * 1024


def dot(a, b):
    return jnp.dot(a, b, preferred_element_type=F32)


def dot_t(a, b):
    return lax.dot_general(a, b, (((1,), (1,)), ((), ())), preferred_element_type=F32)


def running_sum(values):
    lane = lax.broadcasted_iota(jnp.int32, values.shape, 1)
    step = 1
    while step < BLK:
        values = values + jnp.where(lane >= step, pltpu.roll(values, step, 1), 0.0)
        step *= 2
    return values


def columns_of(rows):
    pad = BLK - rows.shape[0]
    return jnp.transpose(jnp.concatenate([rows, jnp.zeros((pad, BLK), F32)], axis=0))


def doc_mask(reset_col, reset_row, strict):
    i = lax.broadcasted_iota(jnp.int32, (BLK, BLK), 0)
    j = lax.broadcasted_iota(jnp.int32, (BLK, BLK), 1)
    below = (i > j) if strict else (i >= j)
    return jnp.where(below & (reset_col == reset_row), 0.0, FAR)


def place_of(part, parts):
    if parts == 1:
        return 0
    odd = lax.rem(lax.axis_index("seq"), 2)
    return odd if part == 1 else 1 - odd


def small_inverses(lower, count):
    lane = lax.broadcasted_iota(jnp.int32, (SUB, BLK), 1)
    packed = []
    for m in lower:
        kept = m[:SUB]
        for b in range(1, BLK // SUB):
            kept = jnp.where(lane // SUB == b, m[b * SUB : (b + 1) * SUB], kept)
        packed.append(kept.astype(BF16))
    packed = jnp.concatenate(packed, axis=0)
    i = lax.broadcasted_iota(jnp.int32, (BLK, BLK), 0)
    j = lax.broadcasted_iota(jnp.int32, (BLK, BLK), 1)
    same = i // SUB == j // SUB
    place = lax.broadcasted_iota(jnp.int32, (count, SUB, BLK), 1)
    lanes = lax.broadcasted_iota(jnp.int32, (count, SUB, BLK), 2)
    found = jnp.where(place == lanes % SUB, 1.0, 0.0)
    for m in range(0, SUB, 2):
        spread = [jnp.where(same & (i % SUB == m + d), 1.0, 0.0).astype(BF16) for d in range(2)]
        pair = dot(packed, jnp.concatenate(spread, axis=1)).reshape(count, SUB, 2 * BLK)
        for d in range(2):
            if m + d < SUB - 1:
                found = found - pair[:, :, d * BLK : (d + 1) * BLK] * found[:, m + d : m + d + 1, :]
    return found.astype(BF16)


def odd_rows(matrix, size):
    return jnp.concatenate(
        [matrix[p : p + size] for p in range(size, BLK, 2 * size)], axis=0
    )


def with_odd_rows(matrix, rows, size):
    parts = []
    for p in range(0, BLK, 2 * size):
        parts.append(matrix[p : p + size])
        parts.append(rows[p // 2 : p // 2 + size])
    return jnp.concatenate(parts, axis=0)


def shard_kernel(
    part, parts, per_key, blocks, keys, devices, *refs
):
    if part == 0:
        log_in, rate_in, start_in, k_in, v_in, w_in = refs[:6]
        wu_ref, zc_ref, rows_ref, end_ref, log_ref, rate_ref, start_ref, k_ref, v_ref = refs[6:15]
        w_keep, w_give = refs[15:17]
    else:
        log_ref, rate_ref, start_ref, k_ref, v_ref, wu_ref, zc_ref, rows_ref, end_ref = refs[:9]
    logs, rates, norms, kt, db, keep, state = refs[len(refs) - 7 :] if part else refs[17:24]
    mine = place_of(part, parts)
    small_copies, k_copies, v_copies = [], [], []
    if part == 0:
        small_sems, k_sems, other_sems, v_sems, w_sems = refs[24:]
        for at, (ref, here) in enumerate(
            ((log_in, log_ref), (rate_in, rate_ref), (start_in, start_ref))
        ):
            small_copies.append(pltpu.make_async_copy(ref, here, small_sems.at[at]))
        width = keys * DK
        for place, copies, sems in ((mine, k_copies, k_sems), (1 - mine, v_copies, other_sems)):
            if parts == 1 and copies is v_copies:
                continue
            lanes = pl.ds(pl.multiple_of(place * width, width), width)
            for c in range(blocks):
                at = (slice(c * BLK, (c + 1) * BLK), lanes)
                copies.append(pltpu.make_async_copy(k_in.at[at], k_ref.at[at], sems.at[c]))
        for c in range(blocks):
            span = slice(c * BLK, (c + 1) * BLK)
            v_copies.append(pltpu.make_async_copy(v_in.at[span], v_ref.at[span], v_sems.at[c]))
        w_copies = []
        order = halving_order(devices)
        columns = w_in.shape[1] // devices
        for at, place in enumerate(order):
            first = pl.multiple_of((lax.axis_index("head") ^ place) * columns, columns)
            to, slot = (w_keep, at) if at < devices // 2 else (w_give, at - devices // 2)
            w_copies.append(
                pltpu.make_async_copy(
                    w_in.at[:, pl.ds(first, columns)],
                    to.at[:, slot * columns : (slot + 1) * columns],
                    w_sems.at[at],
                )
            )
        for copy in small_copies + k_copies:
            copy.start()
        for copy in small_copies:
            copy.wait()
    key_lanes = lambda key: pl.ds(pl.multiple_of((mine * keys + key) * DK, DK), DK)
    head_lanes = lambda h: pl.ds(pl.multiple_of((mine * keys * per_key + h) * DV, DV), DV)
    heads = keys * per_key
    count = heads * blocks
    for place in range(parts):

        @pl.when(mine == place)
        def _():
            for h in range(heads):
                head = place * heads + h
                for c in range(blocks):
                    at = h * blocks + c
                    span = slice(c * BLK, (c + 1) * BLK)
                    logs[at : at + 1, :] = log_ref[head : head + 1, span]
                    rates[at : at + 1, :] = rate_ref[head : head + 1, span]

    starts = start_ref[...].astype(F32)
    sums = running_sum(jnp.concatenate([logs[...], starts], axis=0))
    cum, reset = sums[:count], sums[count:]
    inner = []
    for copy in k_copies:
        copy.wait()
    for copy in v_copies:
        copy.start()
    if part == 0:
        for copy in w_copies:
            copy.start()
    for key in range(keys):
        for c in range(blocks):
            rows = k_ref[c * BLK : (c + 1) * BLK, key_lanes(key)]
            flipped = jnp.transpose(rows.astype(F32))
            turned = flipped.astype(BF16)
            kt[key * blocks + c] = turned
            norms[key * blocks + c : key * blocks + c + 1, :] = jnp.sum(
                flipped * flipped, axis=0, keepdims=True
            )
            inner.append(dot(rows, turned))
    reset_cols = columns_of(reset)
    masks = [doc_mask(reset_cols[:, c : c + 1], reset[c : c + 1, :], True) for c in range(blocks)]

    squares = norms[...] + EPS
    squares = jnp.concatenate(
        [squares[(h // per_key) * blocks : (h // per_key + 1) * blocks] for h in range(heads)], axis=0
    )
    scale = lax.rsqrt(squares)
    log_scale = -0.5 * jnp.log(squares)
    resets = jnp.concatenate([reset] * heads, axis=0)
    rate = rates[...]
    last = cum[:, BLK - 1 :]
    last_reset = resets[:, BLK - 1 :]
    left_cols = columns_of(cum + jnp.log(rate) + log_scale)
    right = cum - log_scale
    head_keep = jnp.where(resets == 0.0, jnp.exp(cum), 0.0)
    tail = jnp.where(resets == last_reset, jnp.exp(last - cum), 0.0) * scale
    erase_row = rate * head_keep * scale
    keep[...] = jnp.broadcast_to(jnp.where(last_reset == 0.0, jnp.exp(last), 0.0), (count, BLK))
    rows_ref[0:count, :] = cum
    rows_ref[count : 2 * count, :] = right
    rows_ref[2 * count :, :] = reset

    lower = []
    for at in range(count):
        c = at % blocks
        gap = left_cols[:, at : at + 1] - right[at : at + 1, :] + masks[c]
        lower.append(inner[at // (per_key * blocks) * blocks + c] * jnp.exp(gap))
    packed = small_inverses(lower, count)
    lower = [m.astype(BF16) for m in lower]
    lane = lax.broadcasted_iota(jnp.int32, (SUB, BLK), 1)
    zero = jnp.zeros((SUB, BLK), BF16)
    ones = [jnp.where(lane // SUB == b, 1.0, 0.0).astype(BF16) for b in range(BLK // SUB)]
    inverse = [
        jnp.concatenate([packed[at] * ones[b] for b in range(BLK // SUB)], axis=0)
        for at in range(count)
    ]
    size = SUB
    while size < BLK:
        i = lax.broadcasted_iota(jnp.int32, (BLK // 2, BLK), 0)
        j = lax.broadcasted_iota(jnp.int32, (BLK // 2, BLK), 1)
        reach = jnp.where(j // size == 2 * (i // size), 1.0, 0.0).astype(BF16)
        odd = [odd_rows(t, size) for t in inverse]
        half = [dot(o, m).astype(BF16) * reach for o, m in zip(odd, lower)]
        fresh = [o - dot(f, t).astype(BF16) for o, f, t in zip(odd, half, inverse)]
        inverse = [with_odd_rows(t, f, size) for t, f in zip(inverse, fresh)]
        size *= 2
    for copy in v_copies:
        copy.wait()
    for at in range(count):
        c, h = at % blocks, at // blocks
        key = h // per_key
        span = slice(c * BLK, (c + 1) * BLK)
        t = inverse[at].astype(F32)
        erase = dot(
            (t * erase_row[at : at + 1, :]).astype(BF16), k_ref[span, key_lanes(key)]
        )
        write = dot((t * rate[at : at + 1, :]).astype(BF16), v_ref[span, head_lanes(h)])
        wu_ref[at, :, :DK] = erase.astype(BF16)
        wu_ref[at, :, DK:] = write.astype(BF16)
    for at in range(count):
        c, key = at % blocks, at // (per_key * blocks)
        tailed = (kt[key * blocks + c].astype(F32) * tail[at : at + 1, :]).astype(BF16)
        db[at] = dot(tailed, wu_ref[at]).astype(BF16)

    i = lax.broadcasted_iota(jnp.int32, (DK, DK), 0)
    j = lax.broadcasted_iota(jnp.int32, (DK, DK), 1)
    for h in range(heads):
        state[h, :, :DV] = jnp.zeros((DK, DV), F32)
        state[h, :, DV:] = jnp.where(i == j, 1.0, 0.0)
    for c in range(blocks):
        for h in range(heads):
            now = state[h]
            low = now.astype(BF16)
            at = h * blocks + c
            zc_ref[at] = low
            moved = dot(db[at, :, :DK], low)
            g = keep[at : at + 1, :]
            state[h, :, :DV] = g * now[:, :DV] - moved[:, :DV] + db[at, :, DK:].astype(F32)
            state[h, :, DV:] = g * now[:, DV:] - moved[:, DV:]
    for h in range(heads):
        end_ref[h] = state[h].astype(BF16)
    if part == 0:
        for copy in w_copies:
            copy.wait()


def vmem(shape, dtype):
    return pltpu.VMEM(shape, dtype)


def in_hbm(array):
    return pltpu.with_memory_space_constraint(array, pltpu.HBM)


def in_vmem():
    return pl.BlockSpec(memory_space=pltpu.VMEM)


def shard_pass(part, parts, arrays, heads_here, per_key, devices):
    tokens_here = arrays[3].shape[0]
    heads = heads_here // parts
    keys = heads // per_key
    blocks = tokens_here // BLK
    count = heads * blocks
    wide = DK + DV
    shapes = [
        vmem((count, BLK, wide), BF16),
        vmem((count, DK, wide), BF16),
        vmem((2 * count + blocks, BLK), F32),
        vmem((heads, DK, wide), BF16),
    ]
    scratch = [
        pltpu.VMEM((count, BLK), F32),
        pltpu.VMEM((count, BLK), F32),
        pltpu.VMEM((keys * blocks, BLK), F32),
        pltpu.VMEM((keys * blocks, DK, BLK), BF16),
        pltpu.VMEM((count, DK, wide), BF16),
        pltpu.VMEM((count, BLK), F32),
        pltpu.VMEM((heads, DK, wide), F32),
    ]
    if part == 0:
        depth, wide = arrays[5].shape
        shapes += [vmem(a.shape, a.dtype) for a in arrays[:5]] + [vmem((depth, wide // 2), BF16)] * 2
        scratch += [pltpu.SemaphoreType.DMA((n,)) for n in (3, blocks, blocks, blocks, devices)]
        arrays = [in_hbm(a) for a in arrays]
        space = pltpu.HBM
    else:
        space = pltpu.VMEM
    outs = pl.pallas_call(
        functools.partial(shard_kernel, part, parts, per_key, blocks, keys, devices),
        in_specs=[pl.BlockSpec(memory_space=space)] * len(arrays),
        out_specs=[in_vmem()] * len(shapes),
        out_shape=shapes,
        scratch_shapes=scratch,
        compiler_params=pltpu.CompilerParams(vmem_limit_bytes=24 * MIB),
        cost_estimate=pl.CostEstimate(
            flops=count * 18 * 2 * BLK**3, bytes_accessed=4 * MIB, transcendentals=0
        ),
        name="shard_pass",
    )(*arrays)
    return list(outs[:4]), outs[4:]


def local_kernel(
    part, parts, per_key, blocks, at_key, rows_ref, q_ref, k_ref, gate_ref, gain_ref, wu_ref, zc_ref,
    out_ref, carry_ref, gated_ref,
):
    count = per_key * blocks
    keys = wu_ref.shape[0] // count
    key = place_of(part, parts) * keys + at_key
    narrow = pl.ds(pl.multiple_of(key * DK, DK), DK)
    total = (rows_ref.shape[0] - blocks) // 2
    base = at_key * count
    cum = rows_ref[base : base + count, :]
    right = rows_ref[total + base : total + base + count, :]
    reset = rows_ref[2 * total :, :]
    cols = columns_of(jnp.concatenate([cum, reset], axis=0))
    units, inner, masks = [], [], []
    for c in range(blocks):
        span = slice(c * BLK, (c + 1) * BLK)
        query = q_ref[span, narrow].astype(F32)
        units.append(jnp.sum(query * query, axis=1, keepdims=True) + EPS)
        inner.append(dot_t(q_ref[span, narrow], k_ref[span, narrow]))
        masks.append(doc_mask(cols[:, count + c : count + c + 1], reset[c : c + 1, :], False))
    scores = []
    for at in range(count):
        c = at % blocks
        left = cols[:, at : at + 1] - 0.5 * jnp.log(units[c])
        gap = left - right[at : at + 1, :] + masks[c]
        scores.append((inner[c] * jnp.exp(gap)).astype(BF16))
    seen = [dot(scores[at], wu_ref[base + at]) for at in range(count)]
    for at in range(count):
        c, h = at % blocks, at // blocks
        span = slice(c * BLK, (c + 1) * BLK)
        wide = slice(h * DV, (h + 1) * DV)
        reset_col = cols[:, count + c : count + c + 1]
        keep = jnp.where(reset_col == 0.0, jnp.exp(cols[:, at : at + 1]), 0.0) * lax.rsqrt(units[c])
        g = (keep * q_ref[span, narrow].astype(F32) - seen[at][:, :DK]).astype(BF16)
        both = dot(g, zc_ref[base + at])
        out_ref[span, wide] = both[:, :DV] + seen[at][:, DK:]
        carry_ref[span, wide] = both[:, DV:].astype(BF16)
        first = pl.multiple_of((key * per_key + h) * DV, DV)
        gate = gate_ref[span, pl.ds(first, DV)].astype(F32)
        gated_ref[span, wide] = gain_ref[...] * (gate / (1.0 + jnp.exp(-gate)))


def local_pass(part, parts, at_key, rows, queries, key_rows, out_gate, gain, wu, zc, per_key):
    tokens_here = queries.shape[0]
    blocks = tokens_here // BLK
    count = per_key * blocks
    wide = per_key * DV
    return pl.pallas_call(
        functools.partial(local_kernel, part, parts, per_key, blocks, at_key),
        in_specs=[in_vmem()] * 7,
        out_specs=[in_vmem()] * 3,
        out_shape=[
            vmem((tokens_here, wide), F32),
            vmem((tokens_here, wide), BF16),
            vmem((tokens_here, wide), F32),
        ],
        compiler_params=pltpu.CompilerParams(vmem_limit_bytes=16 * MIB),
        cost_estimate=pl.CostEstimate(
            flops=count * 8 * 2 * BLK**3, bytes_accessed=4 * MIB, transcendentals=0
        ),
        name="local_pass",
    )(rows, queries, key_rows, out_gate, gain, wu, zc)


def norm_kernel(row, per_key, parts, *refs):
    keys_here = (len(refs) - parts - 1) // 3
    outs = refs[:keys_here]
    carries = refs[keys_here : 2 * keys_here]
    gates = refs[2 * keys_here : 3 * keys_here]
    starts, normed_ref = refs[3 * keys_here : -1], refs[-1]
    rows = slice(row, row + normed_ref.shape[0])
    heads = keys_here * per_key // parts
    for key in range(keys_here):
        for h in range(per_key):
            head = key * per_key + h
            span = slice(h * DV, (h + 1) * DV)
            start = starts[head // heads][head % heads]
            seen = outs[key][rows, span] + dot(carries[key][rows, span], start)
            spread = jnp.mean(seen * seen, axis=1, keepdims=True)
            normed = seen * lax.rsqrt(spread + EPS) * gates[key][rows, span]
            normed_ref[:, head * DV : (head + 1) * DV] = normed.astype(BF16)


def norm_pass(row, rows, outs, carries, gates, starts, per_key):
    arrays = (*outs, *carries, *gates, *starts)
    return pl.pallas_call(
        functools.partial(norm_kernel, row, per_key, len(starts)),
        in_specs=[in_vmem()] * len(arrays),
        out_specs=in_vmem(),
        out_shape=vmem((rows, len(outs) * per_key * DV), BF16),
        compiler_params=pltpu.CompilerParams(vmem_limit_bytes=8 * MIB),
        cost_estimate=pl.CostEstimate(flops=rows, bytes_accessed=rows, transcendentals=0),
        name="norm_pass",
    )(*arrays)


def project_kernel(parts, own_ref, got_ref, kept_ref, given_ref, keep_ref, send_ref):
    heads_wide = own_ref.shape[1] // parts
    width = keep_ref.shape[1]
    for to, columns in ((send_ref, slice(width, 2 * width)), (keep_ref, slice(0, width))):
        total = None
        for normed, weight in ((own_ref, kept_ref), (got_ref, given_ref)):
            for part in range(parts):
                top = pl.multiple_of(place_of(part, parts) * heads_wide, heads_wide)
                term = dot(
                    normed[:, part * heads_wide : (part + 1) * heads_wide],
                    weight[pl.ds(top, heads_wide), columns],
                )
                total = term if total is None else total + term
        to[...] = total.astype(to.dtype)


def project(normed, got, weight_kept, weight_got, parts):
    rows, width = normed.shape[0], weight_kept.shape[1] // 2
    return pl.pallas_call(
        functools.partial(project_kernel, parts),
        in_specs=[in_vmem()] * 4,
        out_specs=[in_vmem()] * 2,
        out_shape=[vmem((rows, width), F32), vmem((rows, width), BF16)],
        compiler_params=pltpu.CompilerParams(vmem_limit_bytes=8 * MIB),
        cost_estimate=pl.CostEstimate(flops=rows, bytes_accessed=rows, transcendentals=0),
        name="project",
    )(normed, got, weight_kept, weight_got)


def halving_order(size):
    def split(group, bit):
        if len(group) == 1:
            return group
        kept = [p for p in group if not p & bit]
        return split(kept, 2 * bit) + split([p for p in group if p & bit], 2 * bit)

    return split(list(range(size)), 1)


def composed(state, move, earlier):
    return (dot(move, earlier) + state.astype(F32)).astype(BF16)


def pair_kernel(mine_ref, got_ref, begun_ref, move_ref):
    odd = lax.rem(lax.axis_index("seq"), 2) == 1

    def join(second, first):
        for h in range(begun_ref.shape[0]):
            moved = dot(second[h, :, DV:], first[h])
            begun_ref[h] = (moved[:, :DV] + second[h, :, :DV].astype(F32)).astype(BF16)
            move_ref[h] = moved[:, DV:].astype(BF16)

    @pl.when(odd)
    def _():
        join(mine_ref, got_ref)

    @pl.when(jnp.logical_not(odd))
    def _():
        join(got_ref, mine_ref)


def step_kernel(state_ref, move_ref, earlier_ref, out_ref):
    for h in range(out_ref.shape[0]):
        out_ref[h] = composed(state_ref[h], move_ref[h], earlier_ref[h])


def last_kernel(mine_ref, got_ref, before_ref, turn_ref, near_ref, far_ref, own_ref, other_ref):
    odd = lax.rem(lax.axis_index("seq"), 2) == 1
    pair = lax.div(lax.axis_index("seq"), 2)

    def fill(first, here_ref, then_ref):
        for h in range(own_ref.shape[0]):
            before = before_ref[h]
            here = composed(before, turn_ref[h], far_ref[h])
            here = jnp.where(pair == 2, near_ref[h], here)
            here = jnp.where(pair == 1, before, here)
            here_ref[h] = jnp.where(pair == 0, jnp.zeros_like(here), here)
        for h in range(own_ref.shape[0]):
            then_ref[h] = composed(first[h, :, :DV], first[h, :, DV:], here_ref[h])

    @pl.when(odd)
    def _():
        fill(got_ref, other_ref, own_ref)

    @pl.when(jnp.logical_not(odd))
    def _():
        fill(mine_ref, own_ref, other_ref)


def small_call(kernel, name, outs, *arrays):
    heads = arrays[0].shape[0]
    return pl.pallas_call(
        kernel,
        in_specs=[in_vmem()] * len(arrays),
        out_specs=[in_vmem()] * len(outs),
        out_shape=[vmem(a.shape, a.dtype) for a in outs],
        compiler_params=pltpu.CompilerParams(vmem_limit_bytes=4 * MIB),
        cost_estimate=pl.CostEstimate(
            flops=heads * 4 * DK**3, bytes_accessed=MIB, transcendentals=0
        ),
        name=name,
    )(*arrays)


def step_call(state, move, earlier):
    shape = jax.ShapeDtypeStruct(earlier.shape, BF16)
    return small_call(step_kernel, "step", [shape], state, move, earlier)[0]


def route(axis, target):
    size = lax.axis_size(axis)
    return [(i, target(i)) for i in range(size) if target(i) is not None]


def exchanged(mine, got, work):
    state = jax.ShapeDtypeStruct(mine.shape[:2] + (DV,), BF16)
    begun, move = small_call(pair_kernel, "pair", [state] * 2, mine, got)
    before = lax.ppermute(begun, "seq", route("seq", lambda i: i ^ 2))
    before, move = work([before, move])
    turn = lax.ppermute(move, "seq", route("seq", lambda i: i ^ 2))
    third = step_call(begun, move, before)
    near = lax.ppermute(third, "seq", route("seq", lambda i: i ^ 6 if i // 2 in (1, 2) else i ^ 1))
    far = lax.ppermute(third, "seq", route("seq", lambda i: i ^ 4 if i // 2 in (1, 3) else i ^ 1))
    turn, far = work((turn, far)), work(far)
    own, other = small_call(
        last_kernel, "last", [state] * 2, mine, got, before, turn, near, far
    )
    return own, work(lax.ppermute(other, "seq", route("seq", lambda i: i ^ 1)))


def handed_on(end):
    size = lax.axis_size("seq")
    onward = route("seq", lambda i: i + 1 if i + 1 < size else None)

    def hop(step, state):
        return lax.ppermute(step_call(end[:, :, :DV], end[:, :, DV:], state), "seq", onward)

    return lax.fori_loop(0, size - 1, hop, jnp.zeros(end.shape[:2] + (DV,), BF16))


def assemble_kernel(pieces, *refs):
    kept, got, out_ref = refs[:pieces], refs[pieces : 2 * pieces], refs[-1]
    row = 0
    for keep_ref, got_ref in zip(kept, got):
        rows = got_ref.shape[0]
        out_ref[row : row + rows, :] = (keep_ref[...] + got_ref[...].astype(F32)).astype(BF16)
        row += rows


def assemble(kept, got):
    ends = [sum(piece.shape[0] for piece in got[: at + 1]) for at in range(len(got))]
    out = jax.ShapeDtypeStruct((ends[-1], got[0].shape[1]), BF16)
    last = got[-1].shape[0]
    params = pltpu.CompilerParams(vmem_limit_bytes=8 * MIB)
    first = pl.pallas_call(
        functools.partial(assemble_kernel, len(got) - 1),
        grid=(1,),
        in_specs=[in_vmem()] * (2 * len(got) - 2),
        out_specs=pl.BlockSpec((ends[-2], out.shape[1]), lambda i: (0, 0)),
        out_shape=out,
        compiler_params=params,
        name="assemble",
    )(*kept[:-1], *got[:-1])
    return pl.pallas_call(
        functools.partial(assemble_kernel, 1),
        grid=(1,),
        in_specs=[in_vmem()] * 2 + [pl.BlockSpec(memory_space=pl.ANY)],
        out_specs=pl.BlockSpec((last, out.shape[1]), lambda i: (ends[-2] // last, 0)),
        out_shape=out,
        input_output_aliases={2: 0},
        compiler_params=params,
        name="assemble_last",
    )(kept[-1], got[-1], first)


def local(
    queries, key_rows, value_rows, out_gate, write_rate, log_gate, doc_start, norm_gain, out_weight
):
    tokens_here = queries.shape[0]
    heads_here = value_rows.shape[1] // DV
    keys_here = key_rows.shape[1] // DK
    per_key = heads_here // keys_here
    devices = lax.axis_size("head")
    parts = 2 if lax.axis_size("seq") == 8 and keys_here % 2 == 0 else 1
    keys = keys_here // parts
    starts = doc_start.reshape(tokens_here // BLK, BLK)
    gain = norm_gain.reshape(1, DV)
    queries, out_gate, gain = (
        pltpu.with_memory_space_constraint(a, pltpu.VMEM) for a in (queries, out_gate, gain)
    )
    shards, got = [], None
    held = [log_gate, write_rate, starts, key_rows, value_rows, out_weight]
    for part in range(parts):
        shard, here = shard_pass(part, parts, held, heads_here, per_key, devices)
        shards.append(shard)
        if part == 0:
            held, (weight_kept, weight_given) = here[:5], here[5:]
            nearby_keys = held[3]
            weight_got = lax.ppermute(weight_given, "head", route("head", lambda i: i ^ 1))
            if parts == 2:
                got = lax.ppermute(shard[3], "seq", route("seq", lambda i: i ^ 1))
    outs, carries, gates = [], [], []

    def work(coming):
        at = len(outs)
        if at == keys_here:
            return coming
        wu, zc, rows, _ = shards[at // keys]
        if isinstance(coming, tuple):
            rows, coming = lax.optimization_barrier((rows, coming[0]))
        out, carry, gate = local_pass(
            at // keys, parts, at % keys, rows, queries, nearby_keys, out_gate, gain, wu, zc, per_key
        )
        if isinstance(coming, list):
            move, out = lax.optimization_barrier((coming[1], out))
            before, out = lax.optimization_barrier((coming[0], out))
            coming = [before, move]
        else:
            coming, out, carry, gate = lax.optimization_barrier((coming, out, carry, gate))
        outs.append(out)
        carries.append(carry)
        gates.append(gate)
        return coming

    if parts == 2:
        mine = shards[1][3]
        rows, mine = lax.optimization_barrier((shards[0][2], mine))
        shards[0][2] = rows
        own, back = exchanged(mine, got, work)
        states = [back, own]
    else:
        states = [handed_on(shards[0][3])]
    while len(outs) < keys_here:
        states[0] = work(states[0])

    unit = tokens_here // 16
    sizes = [unit * share for share in (4, 4, 4, 4)]
    firsts = [sum(sizes[:index]) for index in range(len(sizes))]
    normed = [
        norm_pass(first, rows, outs, carries, gates, states, per_key)
        for first, rows in zip(firsts, sizes)
    ]
    kept, arrived = [], []
    for piece in normed:
        across = lax.ppermute(piece, "head", route("head", lambda i: i ^ 1))
        keep, send = project(piece, across, weight_kept, weight_got, parts)
        bit = 2
        while bit < devices:
            got = lax.ppermute(send, "head", route("head", lambda i: i ^ bit))
            bit *= 2
            if bit < devices:
                keep = keep + got.astype(F32)
                width = keep.shape[1] // 2
                send = keep[:, width:].astype(BF16)
                keep = keep[:, :width]
        kept.append(keep)
        arrived.append(got)
    return assemble(kept, arrived)


def solution(mesh):
    placed = (
        P("seq", "head"),
        P("seq", "head"),
        P("seq", "head"),
        P("seq", "head"),
        P("head", "seq"),
        P("head", "seq"),
        P("seq"),
        P(),
        P("head", None),
    )
    return jax.shard_map(
        local, mesh=mesh, in_specs=placed, out_specs=P("seq", "head"), check_vma=False
    )
```

```python
import functools

import jax
import jax.numpy as jnp
from jax import lax
from jax.experimental import pallas as pl
from jax.experimental.pallas import tpu as pltpu
from jax.sharding import PartitionSpec as P

DK = 128
DV = 128
BLK = 128
SUB = 16
EPS = 1e-06
FAR = -1e30
F32 = jnp.float32
BF16 = jnp.bfloat16
MIB = 1024 * 1024


def dot(a, b):
    return jnp.dot(a, b, preferred_element_type=F32)


def dot_t(a, b):
    return lax.dot_general(a, b, (((1,), (1,)), ((), ())), preferred_element_type=F32)


def running_sum(values):
    lane = lax.broadcasted_iota(jnp.int32, values.shape, 1)
    step = 1
    while step < BLK:
        values = values + jnp.where(lane >= step, pltpu.roll(values, step, 1), 0.0)
        step *= 2
    return values


def columns_of(rows):
    pad = BLK - rows.shape[0]
    return jnp.transpose(jnp.concatenate([rows, jnp.zeros((pad, BLK), F32)], axis=0))


def doc_mask(reset_col, reset_row, strict):
    i = lax.broadcasted_iota(jnp.int32, (BLK, BLK), 0)
    j = lax.broadcasted_iota(jnp.int32, (BLK, BLK), 1)
    below = (i > j) if strict else (i >= j)
    return jnp.where(below & (reset_col == reset_row), 0.0, FAR)


def place_of(part, parts):
    if parts == 1:
        return 0
    odd = lax.rem(lax.axis_index("seq"), 2)
    return odd if part == 1 else 1 - odd


def small_inverses(lower, count):
    lane = lax.broadcasted_iota(jnp.int32, (SUB, BLK), 1)
    packed = []
    for m in lower:
        kept = m[:SUB]
        for b in range(1, BLK // SUB):
            kept = jnp.where(lane // SUB == b, m[b * SUB : (b + 1) * SUB], kept)
        packed.append(kept.astype(BF16))
    packed = jnp.concatenate(packed, axis=0)
    i = lax.broadcasted_iota(jnp.int32, (BLK, BLK), 0)
    j = lax.broadcasted_iota(jnp.int32, (BLK, BLK), 1)
    same = i // SUB == j // SUB
    place = lax.broadcasted_iota(jnp.int32, (count, SUB, BLK), 1)
    lanes = lax.broadcasted_iota(jnp.int32, (count, SUB, BLK), 2)
    found = jnp.where(place == lanes % SUB, 1.0, 0.0)
    for m in range(0, SUB, 2):
        spread = [jnp.where(same & (i % SUB == m + d), 1.0, 0.0).astype(BF16) for d in range(2)]
        pair = dot(packed, jnp.concatenate(spread, axis=1)).reshape(count, SUB, 2 * BLK)
        for d in range(2):
            if m + d < SUB - 1:
                found = found - pair[:, :, d * BLK : (d + 1) * BLK] * found[:, m + d : m + d + 1, :]
    return found.astype(BF16)


def odd_rows(matrix, size):
    return jnp.concatenate(
        [matrix[p : p + size] for p in range(size, BLK, 2 * size)], axis=0
    )


def with_odd_rows(matrix, rows, size):
    parts = []
    for p in range(0, BLK, 2 * size):
        parts.append(matrix[p : p + size])
        parts.append(rows[p // 2 : p // 2 + size])
    return jnp.concatenate(parts, axis=0)


def shard_kernel(
    part, parts, per_key, blocks, keys, devices, *refs
):
    if part == 0:
        log_in, rate_in, start_in, k_in, v_in, w_in = refs[:6]
        wu_ref, zc_ref, rows_ref, end_ref, log_ref, rate_ref, start_ref, k_ref, v_ref = refs[6:15]
        w_keep, w_give = refs[15:17]
    else:
        log_ref, rate_ref, start_ref, k_ref, v_ref, wu_ref, zc_ref, rows_ref, end_ref = refs[:9]
    logs, rates, norms, kt, db, keep, state = refs[len(refs) - 7 :] if part else refs[17:24]
    mine = place_of(part, parts)
    small_copies, k_copies, v_copies = [], [], []
    if part == 0:
        small_sems, k_sems, other_sems, v_sems, w_sems = refs[24:]
        for at, (ref, here) in enumerate(
            ((log_in, log_ref), (rate_in, rate_ref), (start_in, start_ref))
        ):
            small_copies.append(pltpu.make_async_copy(ref, here, small_sems.at[at]))
        width = keys * DK
        for place, copies, sems in ((mine, k_copies, k_sems), (1 - mine, v_copies, other_sems)):
            if parts == 1 and copies is v_copies:
                continue
            lanes = pl.ds(pl.multiple_of(place * width, width), width)
            for c in range(blocks):
                at = (slice(c * BLK, (c + 1) * BLK), lanes)
                copies.append(pltpu.make_async_copy(k_in.at[at], k_ref.at[at], sems.at[c]))
        for c in range(blocks):
            span = slice(c * BLK, (c + 1) * BLK)
            v_copies.append(pltpu.make_async_copy(v_in.at[span], v_ref.at[span], v_sems.at[c]))
        w_copies = []
        order = halving_order(devices)
        columns = w_in.shape[1] // devices
        for at, place in enumerate(order):
            first = pl.multiple_of((lax.axis_index("head") ^ place) * columns, columns)
            to, slot = (w_keep, at) if at < devices // 2 else (w_give, at - devices // 2)
            w_copies.append(
                pltpu.make_async_copy(
                    w_in.at[:, pl.ds(first, columns)],
                    to.at[:, slot * columns : (slot + 1) * columns],
                    w_sems.at[at],
                )
            )
        for copy in small_copies + k_copies:
            copy.start()
        for copy in small_copies:
            copy.wait()
    key_lanes = lambda key: pl.ds(pl.multiple_of((mine * keys + key) * DK, DK), DK)
    head_lanes = lambda h: pl.ds(pl.multiple_of((mine * keys * per_key + h) * DV, DV), DV)
    heads = keys * per_key
    count = heads * blocks
    for place in range(parts):

        @pl.when(mine == place)
        def _():
            for h in range(heads):
                head = place * heads + h
                for c in range(blocks):
                    at = h * blocks + c
                    span = slice(c * BLK, (c + 1) * BLK)
                    logs[at : at + 1, :] = log_ref[head : head + 1, span]
                    rates[at : at + 1, :] = rate_ref[head : head + 1, span]

    starts = start_ref[...].astype(F32)
    sums = running_sum(jnp.concatenate([logs[...], starts], axis=0))
    cum, reset = sums[:count], sums[count:]
    inner = []
    for copy in k_copies:
        copy.wait()
    for copy in v_copies:
        copy.start()
    if part == 0:
        for copy in w_copies:
            copy.start()
    for key in range(keys):
        for c in range(blocks):
            rows = k_ref[c * BLK : (c + 1) * BLK, key_lanes(key)]
            flipped = jnp.transpose(rows.astype(F32))
            turned = flipped.astype(BF16)
            kt[key * blocks + c] = turned
            norms[key * blocks + c : key * blocks + c + 1, :] = jnp.sum(
                flipped * flipped, axis=0, keepdims=True
            )
            inner.append(dot(rows, turned))
    reset_cols = columns_of(reset)
    masks = [doc_mask(reset_cols[:, c : c + 1], reset[c : c + 1, :], True) for c in range(blocks)]

    squares = norms[...] + EPS
    squares = jnp.concatenate(
        [squares[(h // per_key) * blocks : (h // per_key + 1) * blocks] for h in range(heads)], axis=0
    )
    scale = lax.rsqrt(squares)
    log_scale = -0.5 * jnp.log(squares)
    resets = jnp.concatenate([reset] * heads, axis=0)
    rate = rates[...]
    last = cum[:, BLK - 1 :]
    last_reset = resets[:, BLK - 1 :]
    left_cols = columns_of(cum + jnp.log(rate) + log_scale)
    right = cum - log_scale
    head_keep = jnp.where(resets == 0.0, jnp.exp(cum), 0.0)
    tail = jnp.where(resets == last_reset, jnp.exp(last - cum), 0.0) * scale
    erase_row = rate * head_keep * scale
    keep[...] = jnp.broadcast_to(jnp.where(last_reset == 0.0, jnp.exp(last), 0.0), (count, BLK))
    rows_ref[0:count, :] = cum
    rows_ref[count : 2 * count, :] = right
    rows_ref[2 * count :, :] = reset

    lower = []
    for at in range(count):
        c = at % blocks
        gap = left_cols[:, at : at + 1] - right[at : at + 1, :] + masks[c]
        lower.append(inner[at // (per_key * blocks) * blocks + c] * jnp.exp(gap))
    packed = small_inverses(lower, count)
    lower = [m.astype(BF16) for m in lower]
    lane = lax.broadcasted_iota(jnp.int32, (SUB, BLK), 1)
    zero = jnp.zeros((SUB, BLK), BF16)
    ones = [jnp.where(lane // SUB == b, 1.0, 0.0).astype(BF16) for b in range(BLK // SUB)]
    inverse = [
        jnp.concatenate([packed[at] * ones[b] for b in range(BLK // SUB)], axis=0)
        for at in range(count)
    ]
    size = SUB
    while size < BLK:
        i = lax.broadcasted_iota(jnp.int32, (BLK // 2, BLK), 0)
        j = lax.broadcasted_iota(jnp.int32, (BLK // 2, BLK), 1)
        reach = jnp.where(j // size == 2 * (i // size), 1.0, 0.0).astype(BF16)
        odd = [odd_rows(t, size) for t in inverse]
        half = [dot(o, m).astype(BF16) * reach for o, m in zip(odd, lower)]
        fresh = [o - dot(f, t).astype(BF16) for o, f, t in zip(odd, half, inverse)]
        inverse = [with_odd_rows(t, f, size) for t, f in zip(inverse, fresh)]
        size *= 2
    for copy in v_copies:
        copy.wait()
    for at in range(count):
        c, h = at % blocks, at // blocks
        key = h // per_key
        span = slice(c * BLK, (c + 1) * BLK)
        t = inverse[at].astype(F32)
        erase = dot(
            (t * erase_row[at : at + 1, :]).astype(BF16), k_ref[span, key_lanes(key)]
        )
        write = dot((t * rate[at : at + 1, :]).astype(BF16), v_ref[span, head_lanes(h)])
        wu_ref[at, :, :DK] = erase.astype(BF16)
        wu_ref[at, :, DK:] = write.astype(BF16)
    for at in range(count):
        c, key = at % blocks, at // (per_key * blocks)
        tailed = (kt[key * blocks + c].astype(F32) * tail[at : at + 1, :]).astype(BF16)
        db[at] = dot(tailed, wu_ref[at]).astype(BF16)

    i = lax.broadcasted_iota(jnp.int32, (DK, DK), 0)
    j = lax.broadcasted_iota(jnp.int32, (DK, DK), 1)
    for h in range(heads):
        state[h, :, :DV] = jnp.zeros((DK, DV), F32)
        state[h, :, DV:] = jnp.where(i == j, 1.0, 0.0)
    for c in range(blocks):
        for h in range(heads):
            now = state[h]
            low = now.astype(BF16)
            at = h * blocks + c
            zc_ref[at] = low
            moved = dot(db[at, :, :DK], low)
            g = keep[at : at + 1, :]
            state[h, :, :DV] = g * now[:, :DV] - moved[:, :DV] + db[at, :, DK:].astype(F32)
            state[h, :, DV:] = g * now[:, DV:] - moved[:, DV:]
    for h in range(heads):
        end_ref[h] = state[h].astype(BF16)
    if part == 0:
        for copy in w_copies:
            copy.wait()


def vmem(shape, dtype):
    return pltpu.VMEM(shape, dtype)


def in_hbm(array):
    return pltpu.with_memory_space_constraint(array, pltpu.HBM)


def in_vmem():
    return pl.BlockSpec(memory_space=pltpu.VMEM)


def shard_pass(part, parts, arrays, heads_here, per_key, devices):
    tokens_here = arrays[3].shape[0]
    heads = heads_here // parts
    keys = heads // per_key
    blocks = tokens_here // BLK
    count = heads * blocks
    wide = DK + DV
    shapes = [
        vmem((count, BLK, wide), BF16),
        vmem((count, DK, wide), BF16),
        vmem((2 * count + blocks, BLK), F32),
        vmem((heads, DK, wide), BF16),
    ]
    scratch = [
        pltpu.VMEM((count, BLK), F32),
        pltpu.VMEM((count, BLK), F32),
        pltpu.VMEM((keys * blocks, BLK), F32),
        pltpu.VMEM((keys * blocks, DK, BLK), BF16),
        pltpu.VMEM((count, DK, wide), BF16),
        pltpu.VMEM((count, BLK), F32),
        pltpu.VMEM((heads, DK, wide), F32),
    ]
    if part == 0:
        depth, wide = arrays[5].shape
        shapes += [vmem(a.shape, a.dtype) for a in arrays[:5]] + [vmem((depth, wide // 2), BF16)] * 2
        scratch += [pltpu.SemaphoreType.DMA((n,)) for n in (3, blocks, blocks, blocks, devices)]
        arrays = [in_hbm(a) for a in arrays]
        space = pltpu.HBM
    else:
        space = pltpu.VMEM
    outs = pl.pallas_call(
        functools.partial(shard_kernel, part, parts, per_key, blocks, keys, devices),
        in_specs=[pl.BlockSpec(memory_space=space)] * len(arrays),
        out_specs=[in_vmem()] * len(shapes),
        out_shape=shapes,
        scratch_shapes=scratch,
        compiler_params=pltpu.CompilerParams(vmem_limit_bytes=24 * MIB),
        cost_estimate=pl.CostEstimate(
            flops=count * 18 * 2 * BLK**3, bytes_accessed=4 * MIB, transcendentals=0
        ),
        name="shard_pass",
    )(*arrays)
    return list(outs[:4]), outs[4:]


def local_kernel(
    part, parts, per_key, blocks, at_key, rows_ref, q_ref, k_ref, gate_ref, gain_ref, wu_ref, zc_ref,
    out_ref, carry_ref, gated_ref,
):
    count = per_key * blocks
    keys = wu_ref.shape[0] // count
    key = place_of(part, parts) * keys + at_key
    narrow = pl.ds(pl.multiple_of(key * DK, DK), DK)
    total = (rows_ref.shape[0] - blocks) // 2
    base = at_key * count
    cum = rows_ref[base : base + count, :]
    right = rows_ref[total + base : total + base + count, :]
    reset = rows_ref[2 * total :, :]
    cols = columns_of(jnp.concatenate([cum, reset], axis=0))
    units, inner, masks = [], [], []
    for c in range(blocks):
        span = slice(c * BLK, (c + 1) * BLK)
        query = q_ref[span, narrow].astype(F32)
        units.append(jnp.sum(query * query, axis=1, keepdims=True) + EPS)
        inner.append(dot_t(q_ref[span, narrow], k_ref[span, narrow]))
        masks.append(doc_mask(cols[:, count + c : count + c + 1], reset[c : c + 1, :], False))
    scores = []
    for at in range(count):
        c = at % blocks
        left = cols[:, at : at + 1] - 0.5 * jnp.log(units[c])
        gap = left - right[at : at + 1, :] + masks[c]
        scores.append((inner[c] * jnp.exp(gap)).astype(BF16))
    seen = [dot(scores[at], wu_ref[base + at]) for at in range(count)]
    for at in range(count):
        c, h = at % blocks, at // blocks
        span = slice(c * BLK, (c + 1) * BLK)
        wide = slice(h * DV, (h + 1) * DV)
        reset_col = cols[:, count + c : count + c + 1]
        keep = jnp.where(reset_col == 0.0, jnp.exp(cols[:, at : at + 1]), 0.0) * lax.rsqrt(units[c])
        g = (keep * q_ref[span, narrow].astype(F32) - seen[at][:, :DK]).astype(BF16)
        both = dot(g, zc_ref[base + at])
        out_ref[span, wide] = both[:, :DV] + seen[at][:, DK:]
        carry_ref[span, wide] = both[:, DV:].astype(BF16)
        first = pl.multiple_of((key * per_key + h) * DV, DV)
        gate = gate_ref[span, pl.ds(first, DV)].astype(F32)
        gated_ref[span, wide] = gain_ref[...] * (gate / (1.0 + jnp.exp(-gate)))


def local_pass(part, parts, at_key, rows, queries, key_rows, out_gate, gain, wu, zc, per_key):
    tokens_here = queries.shape[0]
    blocks = tokens_here // BLK
    count = per_key * blocks
    wide = per_key * DV
    return pl.pallas_call(
        functools.partial(local_kernel, part, parts, per_key, blocks, at_key),
        in_specs=[in_vmem()] * 7,
        out_specs=[in_vmem()] * 3,
        out_shape=[
            vmem((tokens_here, wide), F32),
            vmem((tokens_here, wide), BF16),
            vmem((tokens_here, wide), F32),
        ],
        compiler_params=pltpu.CompilerParams(vmem_limit_bytes=16 * MIB),
        cost_estimate=pl.CostEstimate(
            flops=count * 8 * 2 * BLK**3, bytes_accessed=4 * MIB, transcendentals=0
        ),
        name="local_pass",
    )(rows, queries, key_rows, out_gate, gain, wu, zc)


def norm_kernel(row, per_key, parts, *refs):
    keys_here = (len(refs) - parts - 1) // 3
    outs = refs[:keys_here]
    carries = refs[keys_here : 2 * keys_here]
    gates = refs[2 * keys_here : 3 * keys_here]
    starts, normed_ref = refs[3 * keys_here : -1], refs[-1]
    rows = slice(row, row + normed_ref.shape[0])
    heads = keys_here * per_key // parts
    for key in range(keys_here):
        for h in range(per_key):
            head = key * per_key + h
            span = slice(h * DV, (h + 1) * DV)
            start = starts[head // heads][head % heads]
            seen = outs[key][rows, span] + dot(carries[key][rows, span], start)
            spread = jnp.mean(seen * seen, axis=1, keepdims=True)
            normed = seen * lax.rsqrt(spread + EPS) * gates[key][rows, span]
            normed_ref[:, head * DV : (head + 1) * DV] = normed.astype(BF16)


def norm_pass(row, rows, outs, carries, gates, starts, per_key):
    arrays = (*outs, *carries, *gates, *starts)
    return pl.pallas_call(
        functools.partial(norm_kernel, row, per_key, len(starts)),
        in_specs=[in_vmem()] * len(arrays),
        out_specs=in_vmem(),
        out_shape=vmem((rows, len(outs) * per_key * DV), BF16),
        compiler_params=pltpu.CompilerParams(vmem_limit_bytes=8 * MIB),
        cost_estimate=pl.CostEstimate(flops=rows, bytes_accessed=rows, transcendentals=0),
        name="norm_pass",
    )(*arrays)


def project_kernel(parts, own_ref, got_ref, kept_ref, given_ref, keep_ref, send_ref):
    heads_wide = own_ref.shape[1] // parts
    width = keep_ref.shape[1]
    for to, columns in ((send_ref, slice(width, 2 * width)), (keep_ref, slice(0, width))):
        total = None
        for normed, weight in ((own_ref, kept_ref), (got_ref, given_ref)):
            for part in range(parts):
                top = pl.multiple_of(place_of(part, parts) * heads_wide, heads_wide)
                term = dot(
                    normed[:, part * heads_wide : (part + 1) * heads_wide],
                    weight[pl.ds(top, heads_wide), columns],
                )
                total = term if total is None else total + term
        to[...] = total.astype(to.dtype)


def project(normed, got, weight_kept, weight_got, parts):
    rows, width = normed.shape[0], weight_kept.shape[1] // 2
    return pl.pallas_call(
        functools.partial(project_kernel, parts),
        in_specs=[in_vmem()] * 4,
        out_specs=[in_vmem()] * 2,
        out_shape=[vmem((rows, width), F32), vmem((rows, width), BF16)],
        compiler_params=pltpu.CompilerParams(vmem_limit_bytes=8 * MIB),
        cost_estimate=pl.CostEstimate(flops=rows, bytes_accessed=rows, transcendentals=0),
        name="project",
    )(normed, got, weight_kept, weight_got)


def halving_order(size):
    def split(group, bit):
        if len(group) == 1:
            return group
        kept = [p for p in group if not p & bit]
        return split(kept, 2 * bit) + split([p for p in group if p & bit], 2 * bit)

    return split(list(range(size)), 1)


def composed(state, move, earlier):
    return (dot(move, earlier) + state.astype(F32)).astype(BF16)


def pair_kernel(mine_ref, got_ref, begun_ref, move_ref):
    odd = lax.rem(lax.axis_index("seq"), 2) == 1

    def join(second, first):
        for h in range(begun_ref.shape[0]):
            moved = dot(second[h, :, DV:], first[h])
            begun_ref[h] = (moved[:, :DV] + second[h, :, :DV].astype(F32)).astype(BF16)
            move_ref[h] = moved[:, DV:].astype(BF16)

    @pl.when(odd)
    def _():
        join(mine_ref, got_ref)

    @pl.when(jnp.logical_not(odd))
    def _():
        join(got_ref, mine_ref)


def step_kernel(state_ref, move_ref, earlier_ref, out_ref):
    for h in range(out_ref.shape[0]):
        out_ref[h] = composed(state_ref[h], move_ref[h], earlier_ref[h])


def last_kernel(mine_ref, got_ref, before_ref, turn_ref, near_ref, far_ref, own_ref, other_ref):
    odd = lax.rem(lax.axis_index("seq"), 2) == 1
    pair = lax.div(lax.axis_index("seq"), 2)

    def fill(first, here_ref, then_ref):
        for h in range(own_ref.shape[0]):
            before = before_ref[h]
            here = composed(before, turn_ref[h], far_ref[h])
            here = jnp.where(pair == 2, near_ref[h], here)
            here = jnp.where(pair == 1, before, here)
            here_ref[h] = jnp.where(pair == 0, jnp.zeros_like(here), here)
        for h in range(own_ref.shape[0]):
            then_ref[h] = composed(first[h, :, :DV], first[h, :, DV:], here_ref[h])

    @pl.when(odd)
    def _():
        fill(got_ref, other_ref, own_ref)

    @pl.when(jnp.logical_not(odd))
    def _():
        fill(mine_ref, own_ref, other_ref)


def small_call(kernel, name, outs, *arrays):
    heads = arrays[0].shape[0]
    return pl.pallas_call(
        kernel,
        in_specs=[in_vmem()] * len(arrays),
        out_specs=[in_vmem()] * len(outs),
        out_shape=[vmem(a.shape, a.dtype) for a in outs],
        compiler_params=pltpu.CompilerParams(vmem_limit_bytes=4 * MIB),
        cost_estimate=pl.CostEstimate(
            flops=heads * 4 * DK**3, bytes_accessed=MIB, transcendentals=0
        ),
        name=name,
    )(*arrays)


def step_call(state, move, earlier):
    shape = jax.ShapeDtypeStruct(earlier.shape, BF16)
    return small_call(step_kernel, "step", [shape], state, move, earlier)[0]


def route(axis, target):
    size = lax.axis_size(axis)
    return [(i, target(i)) for i in range(size) if target(i) is not None]


def exchanged(mine, got, work):
    state = jax.ShapeDtypeStruct(mine.shape[:2] + (DV,), BF16)
    begun, move = small_call(pair_kernel, "pair", [state] * 2, mine, got)
    before = lax.ppermute(begun, "seq", route("seq", lambda i: i ^ 2))
    before, move = work([before, move])
    turn = lax.ppermute(move, "seq", route("seq", lambda i: i ^ 2))
    third = step_call(begun, move, before)
    near = lax.ppermute(third, "seq", route("seq", lambda i: i ^ 6 if i // 2 in (1, 2) else i ^ 1))
    far = lax.ppermute(third, "seq", route("seq", lambda i: i ^ 4 if i // 2 in (1, 3) else i ^ 1))
    turn, far = work((turn, far)), work(far)
    own, other = small_call(
        last_kernel, "last", [state] * 2, mine, got, before, turn, near, far
    )
    return own, work(lax.ppermute(other, "seq", route("seq", lambda i: i ^ 1)))


def handed_on(end):
    size = lax.axis_size("seq")
    onward = route("seq", lambda i: i + 1 if i + 1 < size else None)

    def hop(step, state):
        return lax.ppermute(step_call(end[:, :, :DV], end[:, :, DV:], state), "seq", onward)

    return lax.fori_loop(0, size - 1, hop, jnp.zeros(end.shape[:2] + (DV,), BF16))


def assemble_kernel(pieces, *refs):
    kept, got, out_ref = refs[:pieces], refs[pieces : 2 * pieces], refs[-1]
    row = 0
    for keep_ref, got_ref in zip(kept, got):
        rows = got_ref.shape[0]
        out_ref[row : row + rows, :] = (keep_ref[...] + got_ref[...].astype(F32)).astype(BF16)
        row += rows


def assemble(kept, got):
    ends = [sum(piece.shape[0] for piece in got[: at + 1]) for at in range(len(got))]
    out = jax.ShapeDtypeStruct((ends[-1], got[0].shape[1]), BF16)
    last = got[-1].shape[0]
    params = pltpu.CompilerParams(vmem_limit_bytes=8 * MIB)
    first = pl.pallas_call(
        functools.partial(assemble_kernel, len(got) - 1),
        grid=(1,),
        in_specs=[in_vmem()] * (2 * len(got) - 2),
        out_specs=pl.BlockSpec((ends[-2], out.shape[1]), lambda i: (0, 0)),
        out_shape=out,
        compiler_params=params,
        name="assemble",
    )(*kept[:-1], *got[:-1])
    return pl.pallas_call(
        functools.partial(assemble_kernel, 1),
        grid=(1,),
        in_specs=[in_vmem()] * 2 + [pl.BlockSpec(memory_space=pl.ANY)],
        out_specs=pl.BlockSpec((last, out.shape[1]), lambda i: (ends[-2] // last, 0)),
        out_shape=out,
        input_output_aliases={2: 0},
        compiler_params=params,
        name="assemble_last",
    )(kept[-1], got[-1], first)


def local(
    queries, key_rows, value_rows, out_gate, write_rate, log_gate, doc_start, norm_gain, out_weight
):
    tokens_here = queries.shape[0]
    heads_here = value_rows.shape[1] // DV
    keys_here = key_rows.shape[1] // DK
    per_key = heads_here // keys_here
    devices = lax.axis_size("head")
    parts = 2 if lax.axis_size("seq") == 8 and keys_here % 2 == 0 else 1
    keys = keys_here // parts
    starts = doc_start.reshape(tokens_here // BLK, BLK)
    gain = norm_gain.reshape(1, DV)
    queries, out_gate, gain = (
        pltpu.with_memory_space_constraint(a, pltpu.VMEM) for a in (queries, out_gate, gain)
    )
    shards, got = [], None
    held = [log_gate, write_rate, starts, key_rows, value_rows, out_weight]
    for part in range(parts):
        shard, here = shard_pass(part, parts, held, heads_here, per_key, devices)
        shards.append(shard)
        if part == 0:
            held, (weight_kept, weight_given) = here[:5], here[5:]
            nearby_keys = held[3]
            weight_got = lax.ppermute(weight_given, "head", route("head", lambda i: i ^ 1))
            if parts == 2:
                got = lax.ppermute(shard[3], "seq", route("seq", lambda i: i ^ 1))
    outs, carries, gates = [], [], []

    def work(coming):
        at = len(outs)
        if at == keys_here:
            return coming
        wu, zc, rows, _ = shards[at // keys]
        if isinstance(coming, tuple):
            rows, coming = lax.optimization_barrier((rows, coming[0]))
        out, carry, gate = local_pass(
            at // keys, parts, at % keys, rows, queries, nearby_keys, out_gate, gain, wu, zc, per_key
        )
        if isinstance(coming, list):
            move, out = lax.optimization_barrier((coming[1], out))
            before, out = lax.optimization_barrier((coming[0], out))
            coming = [before, move]
        else:
            coming, out, carry, gate = lax.optimization_barrier((coming, out, carry, gate))
        outs.append(out)
        carries.append(carry)
        gates.append(gate)
        return coming

    if parts == 2:
        mine = shards[1][3]
        rows, mine = lax.optimization_barrier((shards[0][2], mine))
        shards[0][2] = rows
        own, back = exchanged(mine, got, work)
        states = [back, own]
    else:
        states = [handed_on(shards[0][3])]
    while len(outs) < keys_here:
        states[0] = work(states[0])

    unit = tokens_here // 16
    sizes = [unit * share for share in (5, 5, 4, 2)]
    firsts = [sum(sizes[:index]) for index in range(len(sizes))]
    normed = [
        norm_pass(first, rows, outs, carries, gates, states, per_key)
        for first, rows in zip(firsts, sizes)
    ]
    kept, arrived = [], []
    for piece in normed:
        across = lax.ppermute(piece, "head", route("head", lambda i: i ^ 1))
        keep, send = project(piece, across, weight_kept, weight_got, parts)
        bit = 2
        while bit < devices:
            got = lax.ppermute(send, "head", route("head", lambda i: i ^ bit))
            bit *= 2
            if bit < devices:
                keep = keep + got.astype(F32)
                width = keep.shape[1] // 2
                send = keep[:, width:].astype(BF16)
                keep = keep[:, :width]
        kept.append(keep)
        arrived.append(got)
    return assemble(kept, arrived)


def solution(mesh):
    placed = (
        P("seq", "head"),
        P("seq", "head"),
        P("seq", "head"),
        P("seq", "head"),
        P("head", "seq"),
        P("head", "seq"),
        P("seq"),
        P(),
        P("head", None),
    )
    return jax.shard_map(
        local, mesh=mesh, in_specs=placed, out_specs=P("seq", "head"), check_vma=False
    )
```
